512 devices in a mesh: dp: 64 (over x_hi, z, core), pipe: 8 (over y, x_lo).
Axes of the slice: x: 4 (x_hi: 2, x_lo: 2; x = x_hi * 2 + x_lo), y: 4, z: 16, core: 2. Of those that a mesh axis runs over, the one named last changes fastest.
Arguments:
- hidden: bfloat16 [128, 64, 8192], P('dp', None, 'pipe'), may hold values from -14 to 14
- gain: float32 [8192], P('pipe'), may hold values from 0.5 to 1.5
- keys: bfloat16 [128, 8192], P('dp', 'pipe'), may hold values from -0.0625 to 0.0625
- queue: bfloat16 [16384, 8192], P('dp', 'pipe'), may hold values from -1 to 1
- positive: int32 [128], replicated, may hold values from 0 to 127, each once
- mix_rows: int32 [128, 16], replicated, may hold values from 0 to 16383
- mix_weight: float32 [128, 16], replicated, may hold values from 0 to 0.5
Outputs:
- hidden_grad: float32 [128, 64, 8192], P('dp', None, 'pipe')
The draws below stay inside these ranges and needn't reach their ends.
Inputs may be any that keep to these rules, and one draw needn't show every extreme that they name: Every row of keys is the positive of exactly one query.
All inputs are finite; a program needn't handle non-finite values.
Results may differ from the reference program's by a relative error of at most 0.0018.
Values may be sent and summed in bfloat16 or wider, within the bound.
No kernel may reach another device: no remote copies, remote signals or barrier semaphores. Data moves between devices by JAX's collectives and lax.ppermute only.
A program may use at most 64 MiB of HBM per device.

```python
import math
import jax
import jax.numpy as jnp
from jax import lax

D = 8192
S = 64
H = 16
NQ = 128
QUEUE = 16384


def cluster_directions(key):
    number = max(4, QUEUE // 384)
    return jax.random.normal(jax.random.fold_in(key, 23), (number, D), jnp.float32)


def draw_hidden(key, part):
    centres = cluster_directions(key)
    number = centres.shape[0]
    key = jax.random.fold_in(key, 1)
    first = jax.random.fold_in(key, 0)
    third = jax.random.fold_in(key, 2)
    member = jax.random.randint(third, (NQ,), 0, number)
    signal = 0.35 * centres[member][:, None, :]
    values = signal + jax.random.normal(first, (NQ, S, D), jnp.float32)
    return jnp.clip(values, -14.0, 14.0).astype(jnp.bfloat16)


def draw_queue(key, part):
    centres = cluster_directions(key)
    number = centres.shape[0]
    key = jax.random.fold_in(key, 2)
    first = jax.random.fold_in(key, 0)
    fourth = jax.random.fold_in(key, 3)
    fifth = jax.random.fold_in(key, 4)
    unit = D ** (-0.5)
    member = jax.random.randint(fourth, (QUEUE,), 0, number)
    position = jnp.arange(QUEUE, dtype=jnp.float32) / QUEUE
    ceiling = 0.7 * (1.0 + 0.15 * position)
    strength_row = ceiling[:, None] * jnp.exp(jax.random.uniform(fifth, (QUEUE, 1), jnp.float32, math.log(0.05 / 0.7), 0.0))
    signal = strength_row * centres[member]
    values = (signal + jax.random.normal(first, (QUEUE, D), jnp.float32)) * unit
    return jnp.clip(values, -1.0, 1.0).astype(jnp.bfloat16)


def place_ends(array, rng, smallest, largest):
    longest = array.shape.index(max(array.shape))
    spots = []
    for shift in (0, 1):
        where = [jax.random.randint(jax.random.fold_in(rng, axis), (), 0, length) for axis, length in enumerate(array.shape)]
        where[longest] = (where[longest] + shift) % array.shape[longest]
        spots.append(tuple(where))
    return array.at[spots[0]].set(smallest).at[spots[1]].set(largest)


def steps_of(own_key, dims, cuts, smallest, top_value):
    def one(dim, shards_of):
        draws = jax.random.uniform(jax.random.fold_in(jax.random.fold_in(own_key, 6), dim), (shards_of,), jnp.float32, smallest / len(cuts), top_value / len(cuts))
        return jnp.repeat(jnp.exp(draws), dims[dim] // shards_of).reshape((-1,) + (1,) * (len(dims) - dim - 1))

    level = one(*cuts[0])
    for cut in cuts[1:]:
        level = level * one(*cut)
    return level


def normal_values(key, extent, width, limit, cuts=(), kind=jnp.bfloat16):
    factor_of = steps_of(key, extent, cuts, -0.22, 0.18) if cuts else 1.0
    entries = jax.random.normal(key, extent, jnp.float32) * width * factor_of
    return jnp.minimum(jnp.maximum(entries, -limit), limit).astype(kind)


def setup_inputs(seed: int = 0) -> dict:
    arg_keys = jax.random.split(jax.random.key(seed), 8)
    return {
        "hidden": draw_hidden(jax.random.fold_in(arg_keys[7], 71), 0),
        "gain": jnp.clip(1.0 + 0.1 * jax.random.normal(arg_keys[1], (D,), jnp.float32), 0.5, 1.5),
        "keys": normal_values(arg_keys[2], (NQ, D), (D ** -0.5), 0.0625, ((0, 64), (1, 8))),
        "queue": draw_queue(jax.random.fold_in(arg_keys[7], 71), 0),
        "positive": jax.random.permutation(arg_keys[4], NQ).astype(jnp.int32),
        "mix_rows": place_ends(jax.random.randint(arg_keys[5], (NQ, H), 0, QUEUE), jax.random.fold_in(arg_keys[5], 1), 0, QUEUE - 1).astype(jnp.int32),
        "mix_weight": jnp.clip(jax.random.uniform(arg_keys[6], (NQ, H), jnp.float32, 0.0, 0.5), 0.0, 0.5),
    }


COLDNESS_DIVISOR = 0.05
OBJECTIVE_FACTOR = 2048.0
NORM_EPS = 1e-05
MIX_EPS = 1e-06

def reference(hidden, gain, keys, queue, positive, mix_rows, mix_weight):
    states = hidden.astype(jnp.float32)
    mean_square = lax.optimization_barrier(jnp.mean(states * states, axis=-1, keepdims=True))
    inverse_rms = lax.rsqrt(mean_square + NORM_EPS)
    normed = states * inverse_rms
    pooled = lax.optimization_barrier(jnp.mean(normed * gain, axis=1))
    length = jnp.sqrt(lax.optimization_barrier(jnp.sum(pooled * pooled, axis=-1, keepdims=True)))
    query = pooled / length
    query_half = query.astype(jnp.bfloat16)
    positive_cosine = jnp.dot(query_half, keys.T, preferred_element_type=jnp.float32)
    memory_bank_cosine = jnp.dot(query_half, queue.T, preferred_element_type=jnp.float32)
    queue_square = lax.optimization_barrier(jnp.sum(jnp.square(queue.astype(jnp.float32)), axis=-1))
    cosine = jnp.take_along_axis(memory_bank_cosine, mix_rows, axis=1)
    picked_square = queue_square[mix_rows]
    hardness_share = mix_weight
    upper_part_amount = hardness_share + (1.0 - hardness_share) * cosine
    ball_extent_power_two = hardness_share * hardness_share + (1.0 - hardness_share) ** 2 * picked_square + 2.0 * hardness_share * (1.0 - hardness_share) * cosine + MIX_EPS
    ball_extent = jnp.sqrt(ball_extent_power_two)
    combined_energies = upper_part_amount / (COLDNESS_DIVISOR * ball_extent)
    positive_energies = positive_cosine / COLDNESS_DIVISOR
    memory_bank_energies = memory_bank_cosine / COLDNESS_DIVISOR
    row_top = jnp.maximum(jnp.maximum(lax.optimization_barrier(jnp.max(positive_energies, 1)), lax.optimization_barrier(jnp.max(memory_bank_energies, 1))), lax.optimization_barrier(jnp.max(combined_energies, 1)))[:, None]
    total = lax.optimization_barrier(jnp.sum(jnp.exp(positive_energies - row_top), 1)) + lax.optimization_barrier(jnp.sum(jnp.exp(memory_bank_energies - row_top), 1)) + lax.optimization_barrier(jnp.sum(jnp.exp(combined_energies - row_top), 1))
    log_norm = row_top + jnp.log(total)[:, None]
    target = (positive[:, None] == jnp.arange(NQ, dtype=jnp.int32)[None, :]).astype(jnp.float32)
    positive_chance = jnp.exp(positive_energies - log_norm) - target
    memory_bank_chance = jnp.exp(memory_bank_energies - log_norm)
    mixed_prob = jnp.exp(combined_energies - log_norm)
    derivative_rate = (1.0 - hardness_share - upper_part_amount * hardness_share * (1.0 - hardness_share) / ball_extent_power_two) / (COLDNESS_DIVISOR * ball_extent)
    row_index = jnp.arange(NQ, dtype=jnp.int32)[:, None]
    extra_summand = jnp.zeros((NQ, QUEUE), jnp.float32).at[row_index, mix_rows].add(mixed_prob * derivative_rate)
    positive_factor = (OBJECTIVE_FACTOR / COLDNESS_DIVISOR * positive_chance).astype(jnp.bfloat16)
    memory_bank_factor = (OBJECTIVE_FACTOR * (memory_bank_chance / COLDNESS_DIVISOR + extra_summand)).astype(jnp.bfloat16)
    query_grad = jnp.dot(positive_factor, keys, preferred_element_type=jnp.float32) + jnp.dot(memory_bank_factor, queue, preferred_element_type=jnp.float32)
    along = lax.optimization_barrier(jnp.sum(query * query_grad, axis=-1, keepdims=True))
    scaled_grad = gain * (query_grad - along * query) / length
    inner = lax.optimization_barrier(jnp.mean(scaled_grad[:, None, :] * normed, axis=-1, keepdims=True))
    return inverse_rms * (scaled_grad[:, None, :] - normed * inner) / S
```

```python
import functools

import jax
import jax.numpy as jnp
from jax import lax
from jax.experimental import pallas as pl
from jax.experimental.pallas import tpu as pltpu
from jax.sharding import Mesh, PartitionSpec as P

NORM_EPS = 1e-05
MIX_EPS = 1e-06
INV_TEMP = 20.0
LOSS_SCALE = 2048.0
WIDTH = 8192
PART = 1024
CHUNKS = 8
SEQ = 64
TOKENS = 128
QUERIES = 128
ROWS = 256
BANK = 264
SLOTS = 16
EXT = 1152
PIPE = ("y", "xl")
VMEM = 24 << 20

f32 = jnp.float32
bf16 = jnp.bfloat16


def dot_t(a, b):
    return lax.dot_general(a, b, (((1,), (1,)), ((), ())), preferred_element_type=f32)


def split(a):
    hi = a.astype(bf16)
    return hi, (a - hi.astype(f32)).astype(bf16)


def iota(shape, dim):
    return lax.broadcasted_iota(jnp.int32, shape, dim)


def diagonal(square):
    n = square.shape[0]
    on = iota((n, n), 0) == iota((n, n), 1)
    return jnp.sum(jnp.where(on, square, 0.0), axis=0, keepdims=True)


def column(row):
    on = iota((128, 128), 0) == iota((128, 128), 1)
    return jnp.sum(jnp.where(on, row, 0.0), axis=1, keepdims=True)


def fold(row):
    return jnp.concatenate([row[:, c * 128:(c + 1) * 128] for c in range(CHUNKS)], axis=0)


def unfold(block):
    return jnp.concatenate([block[c:c + 1] for c in range(CHUNKS)], axis=1)


def call(kernel, outs, *args, smem=(), scratch=()):
    specs = [
        pl.BlockSpec(memory_space=pltpu.SMEM if i in smem else pltpu.VMEM) for i in range(len(args))
    ]
    many = isinstance(outs, (list, tuple))
    out_specs = [pl.BlockSpec(memory_space=pltpu.VMEM)] * len(outs) if many else pl.BlockSpec(memory_space=pltpu.VMEM)
    return pl.pallas_call(
        kernel,
        out_shape=outs,
        in_specs=specs,
        out_specs=out_specs,
        scratch_shapes=scratch,
        compiler_params=pltpu.CompilerParams(vmem_limit_bytes=VMEM),
    )(*args)


def squares_kernel(hidden_ref, queue_ref, gain_ref, out_ref):
    x = hidden_ref[...]
    weighted = x.astype(f32) * (gain_ref[...] * gain_ref[...])
    hi, lo = split(weighted)
    gram = dot_t(x, hi) + dot_t(x, lo)
    packed = jnp.where(iota((SEQ, 128), 1) < SEQ, gram[:SEQ], gram[SEQ:])
    token = diagonal(dot_t(x, x))
    low = queue_ref[:128]
    high = queue_ref[128:]
    first = diagonal(dot_t(low, low))
    second = diagonal(dot_t(high, high))
    row = iota((8, 128), 0)
    sums = jnp.where(row == 0, token, jnp.where(row == 1, first, jnp.where(row == 2, second, 0.0)))
    for peer in range(8):
        out_ref[peer, :SEQ] = packed
        out_ref[peer, SEQ:] = sums


def query_kernel(sums_ref, hidden_ref, gain_ref, keys_ref, payload_ref, query_ref, stat_ref):
    total = sums_ref[0]
    for peer in range(1, 8):
        total = total + sums_ref[peer]
    token = total[SEQ:SEQ + 1]
    inverse = lax.rsqrt(token / WIDTH + NORM_EPS)
    inverse_column = column(inverse)
    lane = iota((SEQ, 128), 1)
    pair = jnp.where(lane < SEQ, inverse_column[:SEQ], inverse_column[SEQ:]) * inverse
    square = jnp.sum(pair * total[:SEQ], axis=0, keepdims=True)
    first = iota((1, 128), 1) < SEQ
    lengths = [
        jnp.sqrt(jnp.sum(jnp.where(first, square, 0.0), axis=1, keepdims=True)) / SEQ,
        jnp.sqrt(jnp.sum(jnp.where(first, 0.0, square), axis=1, keepdims=True)) / SEQ,
    ]
    weighted = hidden_ref[...].astype(f32) * inverse_column
    gain = gain_ref[...]
    blocks = []
    for q in range(2):
        pooled = jnp.sum(weighted[q * SEQ:(q + 1) * SEQ], axis=0, keepdims=True) * gain / SEQ
        query = pooled / lengths[q]
        query_ref[q:q + 1] = query
        blocks.append(fold(query))
    half = jnp.concatenate(blocks, axis=0).astype(bf16)
    for z in range(16):
        payload_ref[z, :16] = half
        payload_ref[z, 16:] = keys_ref[...]
    length_row = jnp.where(first, lengths[0], lengths[1])
    row = iota((8, 128), 0)
    stat_ref[...] = jnp.where(
        row == 0,
        inverse,
        jnp.where(
            row == 1, total[SEQ + 1:SEQ + 2], jnp.where(row == 2, total[SEQ + 2:SEQ + 3], length_row)
        ),
    )


def score_kernel(gathered_ref, queue_ref, keys_ref, out_ref, rows_ref):
    rows_ref[...] = gathered_ref[:, :16, :].astype(f32).reshape(QUERIES * CHUNKS, 128)
    queries = jnp.concatenate(
        [rows_ref[pl.ds(c, QUERIES, stride=CHUNKS), :].astype(bf16) for c in range(CHUNKS)], axis=1
    )
    queue_dots = dot_t(queue_ref[...], queries)
    key_dots = dot_t(keys_ref[...], queries)[:8]
    for peer in range(8):
        out_ref[peer, :ROWS] = queue_dots
        out_ref[peer, ROWS:] = key_dots


def grad_kernel(dots_ref, stat_ref, queue_ref, keys_ref, pick_ref, weight_ref, target_ref, out_ref):
    dots = dots_ref[0]
    for peer in range(1, 8):
        dots = dots + dots_ref[peer]
    queue_dots = dots[:ROWS]
    key_dots = dots[ROWS:]
    square = jnp.concatenate([column(stat_ref[1:2]), column(stat_ref[2:3])], axis=0)
    index = iota((ROWS, 128), 0)
    pick = pick_ref[...]
    cosines, squares = [], []
    for h in range(SLOTS):
        on = index == pick[h:h + 1]
        cosines.append(jnp.sum(jnp.where(on, queue_dots, 0.0), axis=0, keepdims=True))
        squares.append(jnp.sum(jnp.where(on, square, 0.0), axis=0, keepdims=True))
    cosine = jnp.concatenate(cosines, axis=0)
    picked = jnp.concatenate(squares, axis=0)
    present = (pick >= 0) & (pick < ROWS)
    beta = weight_ref[...]
    rest = 1.0 - beta
    numer = beta + rest * cosine
    radius_sq = beta * beta + rest * rest * picked + 2.0 * beta * rest * cosine + MIX_EPS
    radius_sq = jnp.where(present, radius_sq, 1.0)
    radius = jnp.sqrt(radius_sq)
    mixed = numer * INV_TEMP / radius
    slope = (rest - numer * beta * rest / radius_sq) * INV_TEMP / radius
    low = -1e30
    mixed = jnp.where(present, mixed, low)
    queue_scores = queue_dots * INV_TEMP
    key_row = iota((8, 128), 0)
    key_scores = jnp.where(key_row < 2, key_dots * INV_TEMP, low)
    top = jnp.maximum(
        jnp.maximum(
            jnp.max(queue_scores, axis=0, keepdims=True), jnp.max(key_scores, axis=0, keepdims=True)
        ),
        jnp.max(mixed, axis=0, keepdims=True),
    )
    queue_exp = jnp.exp(queue_scores - top)
    key_exp = jnp.where(key_row < 2, jnp.exp(key_scores - top), 0.0)
    own = key_row == target_ref[...]
    positive = jnp.sum(jnp.where(own, key_exp, 0.0), axis=0, keepdims=True)
    key_exp = jnp.where(own, 0.0, key_exp)
    mixed_exp = jnp.where(present, jnp.exp(mixed - top), 0.0)
    mass = (
        jnp.sum(queue_exp, axis=0, keepdims=True)
        + jnp.sum(key_exp, axis=0, keepdims=True)
        + jnp.sum(mixed_exp, axis=0, keepdims=True)
    )
    extra = jnp.where(present, mixed_exp * slope, 0.0)
    coef = queue_exp * INV_TEMP
    for h in range(SLOTS):
        coef = coef + jnp.where(index == pick[h:h + 1], extra[h:h + 1], 0.0)
    key_coef = jnp.concatenate([key_exp * INV_TEMP, jnp.zeros((8, 128), f32)], axis=0)
    hi, lo = split(jnp.transpose(coef))
    key_hi, key_lo = split(jnp.transpose(jnp.concatenate([key_coef, jnp.zeros((112, 128), f32)], axis=0)))
    bank = queue_ref[...]
    keys = keys_ref[...]
    product = functools.partial(jnp.dot, preferred_element_type=f32)
    out_ref[:, :PART] = (
        product(hi, bank) + product(lo, bank)
        + (product(key_hi[:, :16], keys) + product(key_lo[:, :16], keys))
    )
    lane = iota((128, 128), 1)
    out_ref[:, PART:] = jnp.where(
        lane == 0, column(top), jnp.where(lane == 1, column(mass), jnp.where(lane == 2, column(positive), 0.0))
    )


def merge_kernel(core_ref, pair_ref, out_ref):
    start = pl.multiple_of(core_ref[0] * 64, 64)
    one = pair_ref[0, pl.ds(start, 64), :]
    two = pair_ref[1, pl.ds(start, 64), :]
    top_one = one[:, PART:PART + 1]
    top_two = two[:, PART:PART + 1]
    top = jnp.maximum(top_one, top_two)
    merged = one * jnp.exp(top_one - top) + two * jnp.exp(top_two - top)
    lane = iota((64, EXT), 1)
    merged = jnp.where(lane == PART, top, merged)
    for peer in range(32):
        out_ref[peer] = merged[2 * peer:2 * peer + 2]


def inner_kernel(place_ref, parts_ref, query_ref, gathered_ref, hidden_ref, gain_ref, out_ref, grad_ref):
    stats = parts_ref[:, :, PART:]
    tops = stats[:, :, 0:1]
    top = jnp.max(tops, axis=0, keepdims=True)
    scale = jnp.exp(tops - top)
    total = jnp.sum(parts_ref[...] * scale, axis=0)
    others = total[:, PART + 1:PART + 2]
    full = others + total[:, PART + 2:PART + 3]
    share = others / full
    sums = total[:, :PART] / full
    keys = []
    for q in range(2):
        block = gathered_ref[place_ref[2 * q]].astype(f32)
        keys.append(unfold(jnp.where(place_ref[2 * q + 1] == 0, block[16:24], block[24:32])))
    key = jnp.concatenate(keys, axis=0)
    grad = LOSS_SCALE * (sums - key * (share * INV_TEMP))
    grad_ref[...] = grad
    query = query_ref[...]
    gain = gain_ref[...]
    along = jnp.sum(query * grad, axis=1, keepdims=True)
    rows = jnp.concatenate([grad * gain, query * gain, jnp.zeros((4, PART), f32)], axis=0)
    hi = rows.astype(bf16)
    rest = rows - hi.astype(f32)
    mid = rest.astype(bf16)
    low = (rest - mid.astype(f32)).astype(bf16)
    x = hidden_ref[...]
    dots = dot_t(hi, x) + (dot_t(mid, x) + dot_t(low, x))
    first = iota((1, 128), 1) < SEQ
    of_grad = jnp.where(first, dots[0:1], dots[1:2])
    of_query = jnp.where(first, dots[2:3], dots[3:4])
    of_along = jnp.where(first, along[0:1], along[1:2])
    row = iota((8, 128), 0)
    block = jnp.where(row == 0, of_grad, jnp.where(row == 1, of_query, of_along))
    for peer in range(8):
        out_ref[peer] = block


def output_kernel(sums_ref, grad_ref, query_ref, stat_ref, hidden_ref, gain_ref, out_ref):
    total = sums_ref[0]
    for peer in range(1, 8):
        total = total + sums_ref[peer]
    inverse = stat_ref[0:1]
    length = stat_ref[3:4]
    along = total[2:3]
    inner = inverse * (total[0:1] - along * total[1:2]) / (length * WIDTH)
    inverse_column = column(inverse)
    slide = column(inverse * inverse * inner) / SEQ
    gain = gain_ref[...]
    for q in range(2):
        at = q * SEQ
        scaled = (
            gain * (grad_ref[q:q + 1] - along[:, at:at + 1] * query_ref[q:q + 1])
            / (length[:, at:at + 1] * SEQ)
        )
        out_ref[at:at + SEQ] = (
            inverse_column[at:at + SEQ] * scaled
            - hidden_ref[at:at + SEQ].astype(f32) * slide[at:at + SEQ]
        )


def shape(dims, kind=f32):
    return jax.ShapeDtypeStruct(dims, kind)


def by_device(array):
    rest = array.shape[1:]
    cut = array.reshape((2, 16, 2, 2) + rest)
    order = (2, 0, 1, 3) + tuple(range(4, cut.ndim))
    return cut.transpose(order).reshape((QUERIES,) + rest)


def shards(hidden, gain, keys, queue, positive, mix_rows, mix_weight):
    xh, z, core = lax.axis_index("xh"), lax.axis_index("z"), lax.axis_index("c")
    shard = (xh * 16 + z) * 2 + core
    tokens = hidden.reshape(TOKENS, PART)
    gain = gain.reshape(1, PART)
    pick = by_device(mix_rows).T - shard * ROWS
    weight = by_device(mix_weight).T
    target = by_device(positive).reshape(1, QUERIES) - shard * 2
    mine = lax.dynamic_slice(positive, (shard * 2,), (2,))
    source = mine // 2
    slot = (source % 2) * 32 + source // 2
    place = jnp.stack([slot, mine % 2], axis=1).reshape(4)
    keys_folded = keys.reshape(16, 128)
    keys_padded = jnp.pad(keys, ((0, 14), (0, 0)))

    squares = call(squares_kernel, shape((8, 72, 128)), tokens, queue, gain)
    squares = lax.all_to_all(squares, PIPE, 0, 0)
    payload, query, stat = call(
        query_kernel,
        [shape((16, 32, 128), bf16), shape((2, PART)), shape((8, 128))],
        squares, tokens, gain, keys_folded,
    )
    payload = lax.all_to_all(payload, "z", 0, 0)
    payload = lax.all_gather(payload, "xh")
    gathered = lax.all_gather(payload, "c").reshape(64, 32, 128)
    dots = call(
        score_kernel, shape((8, BANK, 128)), gathered, queue, keys_padded,
        scratch=[pltpu.VMEM((QUERIES * CHUNKS, 128), f32)],
    )
    dots = lax.all_to_all(dots, PIPE, 0, 0)
    parts = call(
        grad_kernel, shape((QUERIES, EXT)), dots, stat, queue, keys_padded, pick, weight, target
    )
    pair = lax.all_gather(parts, "c")
    parts = call(merge_kernel, shape((32, 2, EXT)), core.reshape(1).astype(jnp.int32), pair, smem=(0,))
    parts = lax.all_to_all(parts, ("xh", "z"), 0, 0)
    sums, grad = call(
        inner_kernel,
        [shape((8, 8, 128)), shape((2, PART))],
        place.astype(jnp.int32), parts, query, gathered, tokens, gain, smem=(0,),
    )
    sums = lax.all_to_all(sums, PIPE, 0, 0)
    out = call(output_kernel, shape((TOKENS, PART)), sums, grad, query, stat, tokens, gain)
    return out.reshape(2, SEQ, PART)


def solution(mesh):
    fine = Mesh(mesh.devices.reshape(2, 16, 2, 4, 2), ("xh", "z", "c", "y", "xl"))
    dp = ("xh", "z", "c")
    placed = (P(dp, None, PIPE), P(PIPE), P(dp, PIPE), P(dp, PIPE), P(), P(), P())
    return jax.shard_map(
        shards, mesh=fine, in_specs=placed, out_specs=P(dp, None, PIPE), check_vma=False
    )
```

```python
import functools

import jax
import jax.numpy as jnp
from jax import lax
from jax.experimental import pallas as pl
from jax.experimental.pallas import tpu as pltpu
from jax.sharding import Mesh, PartitionSpec as P

NORM_EPS = 1e-05
MIX_EPS = 1e-06
INV_TEMP = 20.0
LOSS_SCALE = 2048.0
WIDTH = 8192
PART = 1024
CHUNKS = 8
SEQ = 64
TOKENS = 128
QUERIES = 128
ROWS = 256
BANK = 264
SLOTS = 16
EXT = 1152
ABSENT = -30000.0
FINE = 65536.0
FULL = 32000.0
PIPE = ("y", "xl")
VMEM = 24 << 20

f32 = jnp.float32
bf16 = jnp.bfloat16


def dot_t(a, b):
    return lax.dot_general(a, b, (((1,), (1,)), ((), ())), preferred_element_type=f32)


def split(a):
    hi = a.astype(bf16)
    return hi, (a - hi.astype(f32)).astype(bf16)


def iota(shape, dim):
    return lax.broadcasted_iota(jnp.int32, shape, dim)


def padded(keys):
    return jnp.concatenate([keys.astype(f32), jnp.zeros((14, PART), f32)], axis=0).astype(bf16)


def reordered(rows):
    old, new = iota((128, 128), 0), iota((128, 128), 1)
    place = (new % 64) // 2 * 4 + new // 64 * 2 + new % 2
    chosen = jnp.where(old == place, 1.0, 0.0).astype(bf16)
    hi = rows.astype(bf16)
    rest = rows - hi.astype(f32)
    mid = rest.astype(bf16)
    low = (rest - mid.astype(f32)).astype(bf16)
    product = functools.partial(jnp.dot, preferred_element_type=f32)
    return product(hi, chosen) + (product(mid, chosen) + product(low, chosen))


def whole(a):
    return jnp.floor(a + 0.5).astype(jnp.int32)


def diagonal(square):
    n = square.shape[0]
    on = iota((n, n), 0) == iota((n, n), 1)
    return jnp.sum(jnp.where(on, square, 0.0), axis=0, keepdims=True)


def column(row):
    on = iota((128, 128), 0) == iota((128, 128), 1)
    return jnp.sum(jnp.where(on, row, 0.0), axis=1, keepdims=True)


def fold(row):
    return jnp.concatenate([row[:, c * 128:(c + 1) * 128] for c in range(CHUNKS)], axis=0)


def unfold(block):
    return jnp.concatenate([block[c:c + 1] for c in range(CHUNKS)], axis=1)


def call(kernel, outs, *args, smem=(), far=(), scratch=()):
    def space(i):
        return pltpu.SMEM if i in smem else pltpu.HBM if i in far else pltpu.VMEM

    specs = [pl.BlockSpec(memory_space=space(i)) for i in range(len(args))]
    many = isinstance(outs, (list, tuple))
    out_specs = [pl.BlockSpec(memory_space=pltpu.VMEM)] * len(outs) if many else pl.BlockSpec(memory_space=pltpu.VMEM)
    return pl.pallas_call(
        kernel,
        out_shape=outs,
        in_specs=specs,
        out_specs=out_specs,
        scratch_shapes=scratch,
        compiler_params=pltpu.CompilerParams(vmem_limit_bytes=VMEM),
    )(*args)


def squares_kernel(ids_ref, hidden_far, queue_far, gain_far, out_ref, hidden_ref, queue_ref, gain_ref, sems):
    copies = [
        pltpu.make_async_copy(gain_far, gain_ref, sems.at[0]),
        pltpu.make_async_copy(hidden_far, hidden_ref, sems.at[1]),
        pltpu.make_async_copy(queue_far, queue_ref, sems.at[2]),
    ]
    for copy in copies:
        copy.start()
    copies[0].wait()
    copies[1].wait()
    x = hidden_ref[...]
    weighted = x.astype(f32) * (gain_ref[...] * gain_ref[...])
    hi, lo = split(weighted)
    gram = dot_t(x, hi) + dot_t(x, lo)
    up = iota((SEQ, 128), 0) < iota((SEQ, 128), 1)
    both = jnp.where(up, gram[:SEQ], pltpu.roll(gram[SEQ:], SEQ, 1))
    left = iota((32, 128), 1) < SEQ
    packed = jnp.where(left, both[:32], pltpu.roll(both[32:], SEQ, 1))
    token = diagonal(dot_t(x, x))
    diag = diagonal(gram)
    copies[2].wait()
    low = queue_ref[:128]
    high = queue_ref[128:]
    first = diagonal(dot_t(low, low))
    second = diagonal(dot_t(high, high))
    row = iota((8, 128), 0)
    sums = jnp.where(
        row == 0,
        token,
        jnp.where(row == 1, first, jnp.where(row == 2, second, jnp.where(row == 3, diag, 0.0))),
    )
    for peer in range(8):
        out_ref[peer, :32] = packed
        out_ref[peer, 32:] = sums


def query_kernel(sums_ref, hidden_ref, gain_ref, keys_ref, payload_ref, query_ref, stat_ref):
    total = sums_ref[0]
    for peer in range(1, 8):
        total = total + sums_ref[peer]
    token = total[32:33]
    diag = total[35:36]
    inverse = lax.rsqrt(token / WIDTH + NORM_EPS)
    inverse_column = column(inverse)
    first = iota((1, 128), 1) < SEQ
    both = jnp.concatenate([total[:32], pltpu.roll(total[:32], SEQ, 1)], axis=0)
    t, u = iota((SEQ, 128), 0), iota((SEQ, 128), 1)
    second = pltpu.roll(jnp.broadcast_to(inverse, (8, 128)), SEQ, 1)[:1]
    pair = jnp.where(t < u, inverse_column[:SEQ] * inverse, inverse_column[SEQ:] * second)
    pair = jnp.where((t != u) & (u < SEQ), pair * both, 0.0)
    own = diag * inverse * inverse
    lengths = []
    for mask, on in ((first, t < u), (jnp.logical_not(first), t > u)):
        off = jnp.sum(jnp.where(on, pair, 0.0), axis=0, keepdims=True)
        square = jnp.sum(2.0 * off + jnp.where(mask, own, 0.0), axis=1, keepdims=True)
        lengths.append(jnp.sqrt(square) / SEQ)
    weighted = hidden_ref[...].astype(f32) * inverse_column
    gain = gain_ref[...]
    blocks = []
    for q in range(2):
        pooled = jnp.sum(weighted[q * SEQ:(q + 1) * SEQ], axis=0, keepdims=True) * gain / SEQ
        query = pooled / lengths[q]
        query_ref[q:q + 1] = query
        blocks.append(fold(query))
    keys = keys_ref[...].astype(f32)
    blocks += [fold(keys[0:1]), fold(keys[1:2])]
    half = jnp.concatenate(blocks, axis=0).astype(bf16)
    for z in range(16):
        payload_ref[z] = half
    length_row = jnp.where(first, lengths[0], lengths[1])
    row = iota((8, 128), 0)
    stat_ref[...] = jnp.where(
        row == 0,
        inverse,
        jnp.where(row == 1, total[33:34], jnp.where(row == 2, total[34:35], length_row)),
    )


def score_kernel(gathered_ref, queue_ref, keys_ref, out_ref, rows_ref):
    rows_ref[...] = gathered_ref[:, :16, :].astype(f32).reshape(QUERIES * CHUNKS, 128)
    queries = jnp.concatenate(
        [rows_ref[pl.ds(c, QUERIES, stride=CHUNKS), :].astype(bf16) for c in range(CHUNKS)], axis=1
    )
    queue_dots = dot_t(queue_ref[...], queries)
    key_dots = dot_t(padded(keys_ref[...]), queries)[:8]
    for peer in range(8):
        out_ref[peer, :ROWS] = queue_dots
        out_ref[peer, ROWS:] = key_dots


def grad_kernel(
    ids_ref, dots_ref, stat_ref, queue_ref, keys_ref, pick_ref, weight_ref, target_ref, keep_ref, send_ref, all_ref
):
    dots = dots_ref[0]
    for peer in range(1, 8):
        dots = dots + dots_ref[peer]
    queue_dots = dots[:ROWS]
    key_dots = dots[ROWS:]
    square = jnp.concatenate([column(stat_ref[1:2]), column(stat_ref[2:3])], axis=0)
    index = iota((ROWS, 128), 0)
    indices = jnp.concatenate(
        [
            pick_ref[...].astype(f32),
            weight_ref[...],
            jnp.broadcast_to(target_ref[...].astype(f32), (8, 128)),
        ],
        axis=0,
    )
    indices = reordered(indices)
    shard = ids_ref[0]
    pick = whole(indices[:16]) - shard * ROWS
    beta = indices[16:32]
    target = whole(indices[32:33]) - shard * 2
    cosines, squares = [], []
    for h in range(SLOTS):
        on = index == pick[h:h + 1]
        cosines.append(jnp.sum(jnp.where(on, queue_dots, 0.0), axis=0, keepdims=True))
        squares.append(jnp.sum(jnp.where(on, square, 0.0), axis=0, keepdims=True))
    cosine = jnp.concatenate(cosines, axis=0)
    picked = jnp.concatenate(squares, axis=0)
    present = (pick >= 0) & (pick < ROWS)
    rest = 1.0 - beta
    numer = beta + rest * cosine
    radius_sq = beta * beta + rest * rest * picked + 2.0 * beta * rest * cosine + MIX_EPS
    radius_sq = jnp.where(present, radius_sq, 1.0)
    radius = jnp.sqrt(radius_sq)
    mixed = numer * INV_TEMP / radius
    slope = (rest - numer * beta * rest / radius_sq) * INV_TEMP / radius
    low = -1e30
    mixed = jnp.where(present, mixed, low)
    queue_scores = queue_dots * INV_TEMP
    key_row = iota((8, 128), 0)
    own = key_row == target
    held = (target >= 0) & (target < 2)
    positive = jnp.sum(jnp.where(own, key_dots * INV_TEMP, 0.0), axis=0, keepdims=True)
    positive = jnp.where(held, positive, ABSENT)
    other = (key_row < 2) & jnp.logical_not(own)
    key_scores = jnp.where(other, key_dots * INV_TEMP, low)
    top = jnp.maximum(
        jnp.maximum(
            jnp.max(queue_scores, axis=0, keepdims=True), jnp.max(key_scores, axis=0, keepdims=True)
        ),
        jnp.max(mixed, axis=0, keepdims=True),
    )
    queue_exp = jnp.exp(queue_scores - top)
    key_exp = jnp.where(other, jnp.exp(key_scores - top), 0.0)
    mixed_exp = jnp.where(present, jnp.exp(mixed - top), 0.0)
    mass = (
        jnp.sum(queue_exp, axis=0, keepdims=True)
        + jnp.sum(key_exp, axis=0, keepdims=True)
        + jnp.sum(mixed_exp, axis=0, keepdims=True)
    )
    extra = jnp.where(present, mixed_exp * slope, 0.0)
    coef = queue_exp * INV_TEMP
    for h in range(SLOTS):
        coef = coef + jnp.where(index == pick[h:h + 1], extra[h:h + 1], 0.0)
    key_coef = jnp.concatenate([key_exp * INV_TEMP, jnp.zeros((8, 128), f32)], axis=0)
    hi, lo = split(jnp.transpose(coef))
    key_hi, key_lo = split(jnp.transpose(jnp.concatenate([key_coef, jnp.zeros((112, 128), f32)], axis=0)))
    bank = queue_ref[...]
    keys = padded(keys_ref[...])
    product = functools.partial(jnp.dot, preferred_element_type=f32)
    all_ref[:, :PART] = (
        product(hi, bank) + product(lo, bank)
        + (product(key_hi[:, :16], keys) + product(key_lo[:, :16], keys))
    )
    lane = iota((128, 128), 1)
    all_ref[:, PART:] = jnp.where(
        lane == 0, column(top), jnp.where(lane == 1, column(mass), jnp.where(lane == 2, column(positive), 0.0))
    )
    core = ids_ref[1]
    keep_ref[...] = all_ref[pl.ds(pl.multiple_of(core * 64, 64), 64), :]
    send_ref[...] = all_ref[pl.ds(pl.multiple_of((1 - core) * 64, 64), 64), :]


def merge_kernel(keep_ref, came_ref, out_ref):
    one = keep_ref[...]
    two = came_ref[...]
    top_one = one[:, PART:PART + 1]
    top_two = two[:, PART:PART + 1]
    top = jnp.maximum(top_one, top_two)
    up_one = jnp.exp(top_one - top)
    up_two = jnp.exp(top_two - top)
    sums = one[:, :PART] * up_one + two[:, :PART] * up_two
    mass = one[:, PART + 1:PART + 2] * up_one + two[:, PART + 1:PART + 2] * up_two
    positive = jnp.maximum(one[:, PART + 2:PART + 3], two[:, PART + 2:PART + 3])
    most = jnp.maximum(jnp.max(jnp.abs(sums), axis=1, keepdims=True), 1e-30)
    level = jnp.floor(jnp.log(most) * FINE + 0.5) / FINE
    out_ref[:, :PART] = whole(sums * (FULL * jnp.exp(-level))).astype(jnp.int16)
    lane = iota((64, 128), 1)
    stats = jnp.where(lane == 0, top, jnp.where(lane == 1, mass, jnp.where(lane == 2, positive, level)))
    pieces = jnp.floor(stats)
    rest = (stats - pieces) * FINE
    middle = jnp.floor(rest)
    last = jnp.floor((rest - middle) * FINE)
    middle = middle - 32768.0
    last = last - 32768.0
    block = jnp.where(lane < 4, pieces, jnp.where(lane < 8, pltpu.roll(middle, 4, 1), pltpu.roll(last, 8, 1)))
    out_ref[:, PART:] = jnp.where(lane < 12, block, 0.0).astype(jnp.int32).astype(jnp.int16)


def inner_kernel(ids_ref, positive_ref, parts_ref, query_ref, gathered_ref, hidden_ref, gain_ref, out_ref, grad_ref):
    pieces = parts_ref[:, PART:].astype(jnp.int32).astype(f32)
    middle = pltpu.roll(pieces, 124, 1) + 32768.0
    last = pltpu.roll(pieces, 120, 1) + 32768.0
    stats = pieces + (middle + last / FINE) / FINE
    tops = stats[:, 0:1]
    positives = stats[:, 2:3]
    even = iota((64, 1), 0) % 2 == 0
    both = jnp.maximum(tops, positives)
    top = jnp.where(
        even,
        jnp.max(jnp.where(even, both, ABSENT), axis=0, keepdims=True),
        jnp.max(jnp.where(even, ABSENT, both), axis=0, keepdims=True),
    )
    scale = jnp.exp(tops - top)
    mass = stats[:, 1:2] * scale
    own = jnp.exp(positives - top)
    weighted = parts_ref[:, :PART].astype(jnp.int32).astype(f32) * (scale * jnp.exp(stats[:, 3:4]) / FULL)
    folded = weighted[:8]
    for block in range(1, 8):
        folded = folded + weighted[8 * block:8 * block + 8]
    folded = (folded[0:2] + folded[2:4]) + (folded[4:6] + folded[6:8])
    others, full = [], []
    for mask in (even, jnp.logical_not(even)):
        others.append(jnp.sum(jnp.where(mask, mass, 0.0), axis=0, keepdims=True))
        full.append(others[-1] + jnp.sum(jnp.where(mask, own, 0.0), axis=0, keepdims=True))
    others = jnp.concatenate(others, axis=0)
    full = jnp.concatenate(full, axis=0)
    share = others / full
    sums = folded / full
    keys = []
    for q in range(2):
        row = positive_ref[2 * ids_ref[0] + q]
        block = gathered_ref[row // 2 % 2 * 32 + row // 4].astype(f32)
        keys.append(unfold(jnp.where(row % 2 == 0, block[16:24], block[24:32])))
    key = jnp.concatenate(keys, axis=0)
    grad = LOSS_SCALE * (sums - key * (share * INV_TEMP))
    grad_ref[...] = grad
    query = query_ref[...]
    gain = gain_ref[...]
    along = jnp.sum(query * grad, axis=1, keepdims=True)
    rows = jnp.concatenate([grad * gain, query * gain, jnp.zeros((4, PART), f32)], axis=0)
    hi = rows.astype(bf16)
    rest = rows - hi.astype(f32)
    mid = rest.astype(bf16)
    low = (rest - mid.astype(f32)).astype(bf16)
    x = hidden_ref[...]
    dots = dot_t(hi, x) + (dot_t(mid, x) + dot_t(low, x))
    first = iota((1, 128), 1) < SEQ
    of_grad = jnp.where(first, dots[0:1], dots[1:2])
    of_query = jnp.where(first, dots[2:3], dots[3:4])
    of_along = jnp.where(first, along[0:1], along[1:2])
    row = iota((8, 128), 0)
    block = jnp.where(row == 0, of_grad, jnp.where(row == 1, of_query, of_along))
    for peer in range(8):
        out_ref[peer] = block


def output_kernel(sums_ref, grad_ref, query_ref, stat_ref, hidden_ref, gain_ref, out_ref):
    total = sums_ref[0]
    for peer in range(1, 8):
        total = total + sums_ref[peer]
    inverse = stat_ref[0:1]
    length = stat_ref[3:4]
    along = total[2:3]
    inner = inverse * (total[0:1] - along * total[1:2]) / (length * WIDTH)
    inverse_column = column(inverse)
    slide = column(inverse * inverse * inner) / SEQ
    gain = gain_ref[...]
    for q in range(2):
        at = q * SEQ
        scaled = (
            gain * (grad_ref[q:q + 1] - along[:, at:at + 1] * query_ref[q:q + 1])
            / (length[:, at:at + 1] * SEQ)
        )
        out_ref[at:at + SEQ] = (
            inverse_column[at:at + SEQ] * scaled
            - hidden_ref[at:at + SEQ].astype(f32) * slide[at:at + SEQ]
        )


def shape(dims, kind=f32):
    return jax.ShapeDtypeStruct(dims, kind)


def shards(hidden, gain, keys, queue, positive, mix_rows, mix_weight):
    xh, z, core = lax.axis_index("xh"), lax.axis_index("z"), lax.axis_index("c")
    shard = (xh * 16 + z) * 2 + core
    tokens = hidden.reshape(TOKENS, PART)
    gain = gain.reshape(1, PART)
    ids = jnp.stack([shard, core]).astype(jnp.int32)

    squares = call(
        squares_kernel, shape((8, 40, 128)), ids, tokens, queue, gain, smem=(0,), far=(1, 2, 3),
        scratch=[
            pltpu.VMEM((TOKENS, PART), bf16),
            pltpu.VMEM((ROWS, PART), bf16),
            pltpu.VMEM((1, PART), f32),
            pltpu.SemaphoreType.DMA((3,)),
        ],
    )
    squares = lax.all_to_all(squares, PIPE, 0, 0)
    payload, query, stat = call(
        query_kernel,
        [shape((16, 32, 128), bf16), shape((2, PART)), shape((8, 128))],
        squares, tokens, gain, keys,
    )
    payload = lax.all_to_all(payload, "z", 0, 0)
    payload = lax.all_gather(payload, "xh")
    gathered = lax.all_gather(payload, "c").reshape(64, 32, 128)
    dots = call(
        score_kernel, shape((8, BANK, 128)), gathered, queue, keys,
        scratch=[pltpu.VMEM((QUERIES * CHUNKS, 128), f32)],
    )
    dots = lax.all_to_all(dots, PIPE, 0, 0)
    half = shape((QUERIES // 2, EXT))
    keep, send = call(
        grad_kernel, [half, half], ids, dots, stat, queue, keys, mix_rows.T, mix_weight.T,
        positive.reshape(1, QUERIES), smem=(0,), scratch=[pltpu.VMEM((QUERIES, EXT), f32)],
    )
    came = lax.ppermute(send, "c", [(0, 1), (1, 0)])
    parts = call(merge_kernel, shape((QUERIES // 2, EXT), jnp.int16), keep, came)
    parts = lax.all_to_all(parts.reshape(32, 2, EXT), ("xh", "z"), 0, 0).reshape(QUERIES // 2, EXT)
    sums, grad = call(
        inner_kernel,
        [shape((8, 8, 128)), shape((2, PART))],
        ids, positive, parts, query, gathered, tokens, gain, smem=(0, 1),
    )
    sums = lax.all_to_all(sums, PIPE, 0, 0)
    out = call(output_kernel, shape((TOKENS, PART)), sums, grad, query, stat, tokens, gain)
    return out.reshape(2, SEQ, PART)


def solution(mesh):
    fine = Mesh(mesh.devices.reshape(2, 16, 2, 4, 2), ("xh", "z", "c", "y", "xl"))
    dp = ("xh", "z", "c")
    placed = (P(dp, None, PIPE), P(PIPE), P(dp, PIPE), P(dp, PIPE), P(), P(), P())
    return jax.shard_map(
        shards, mesh=fine, in_specs=placed, out_specs=P(dp, None, PIPE), check_vma=False
    )
```

```python
import functools

import jax
import jax.numpy as jnp
from jax import lax
from jax.experimental import pallas as pl
from jax.experimental.pallas import tpu as pltpu
from jax.sharding import Mesh, PartitionSpec as P

NORM_EPS = 1e-05
MIX_EPS = 1e-06
INV_TEMP = 20.0
LOSS_SCALE = 2048.0
WIDTH = 8192
PART = 1024
CHUNKS = 8
SEQ = 64
TOKENS = 128
QUERIES = 128
ROWS = 256
KEYS = 16
BANK = ROWS + KEYS
BANKS = 4
OWN = 32
SLOTS = 16
EXT = 2 * PART + 128
ABSENT = -30000.0
FINE = 65536.0
FULL = 32000.0
PIPE = ("y", "xl")
VMEM = 24 << 20

f32 = jnp.float32
bf16 = jnp.bfloat16


def dot_t(a, b):
    return lax.dot_general(a, b, (((1,), (1,)), ((), ())), preferred_element_type=f32)


def split(a):
    hi = a.astype(bf16)
    return hi, (a - hi.astype(f32)).astype(bf16)


def iota(shape, dim):
    return lax.broadcasted_iota(jnp.int32, shape, dim)


def padded(keys):
    return jnp.concatenate([keys.astype(f32), jnp.zeros((KEYS - 2, PART), f32)], axis=0).astype(bf16)


def own_lanes(rows):
    old, new = iota((128, 128), 0), iota((128, 128), 1) % OWN
    place = ((lax.axis_index("xh") * 16 + new // 2) * 2 + lax.axis_index("c")) * 2 + new % 2
    chosen = jnp.where(old == place, 1.0, 0.0).astype(bf16)
    hi = rows.astype(bf16)
    rest = rows - hi.astype(f32)
    mid = rest.astype(bf16)
    low = (rest - mid.astype(f32)).astype(bf16)
    product = functools.partial(jnp.dot, preferred_element_type=f32)
    return product(hi, chosen) + (product(mid, chosen) + product(low, chosen))


def over_banks(op, row):
    block = jnp.broadcast_to(row, (8, 128))
    block = op(block, pltpu.roll(block, 64, 1))
    return op(block, pltpu.roll(block, 32, 1))[:1]


def whole(a):
    return jnp.floor(a + 0.5).astype(jnp.int32)


def diagonal(square):
    n = square.shape[0]
    on = iota((n, n), 0) == iota((n, n), 1)
    return jnp.sum(jnp.where(on, square, 0.0), axis=0, keepdims=True)


def flat(tall):
    on = iota((128, 128), 0) == iota((128, 128), 1)
    return jnp.sum(jnp.where(on, tall, 0.0), axis=0, keepdims=True)


def column(row):
    on = iota((128, 128), 0) == iota((128, 128), 1)
    return jnp.sum(jnp.where(on, row, 0.0), axis=1, keepdims=True)


def fold(row):
    return jnp.concatenate([row[:, c * 128:(c + 1) * 128] for c in range(CHUNKS)], axis=0)


def unfold(block):
    return jnp.concatenate([block[c:c + 1] for c in range(CHUNKS)], axis=1)


def call(kernel, outs, *args, far=(), far_outs=(), scratch=(), vmem=VMEM):
    def place(i, far):
        return pl.BlockSpec(memory_space=pltpu.HBM if i in far else pltpu.VMEM)

    many = isinstance(outs, (list, tuple))
    return pl.pallas_call(
        kernel,
        out_shape=outs,
        in_specs=[place(i, far) for i in range(len(args))],
        out_specs=[place(i, far_outs) for i in range(len(outs))] if many else place(0, far_outs),
        scratch_shapes=scratch,
        compiler_params=pltpu.CompilerParams(vmem_limit_bytes=vmem),
    )(*args)


def squares_kernel(
    hidden_far, queue_far, gain_far, keys_far, out_ref, bank_far, hidden_ref, gain_ref, keys_ref, padded_ref, sems
):
    copies = [
        pltpu.make_async_copy(keys_far, keys_ref, sems.at[0]),
        pltpu.make_async_copy(queue_far, bank_far.at[pl.ds(0, ROWS)], sems.at[1]),
        pltpu.make_async_copy(gain_far, gain_ref, sems.at[2]),
        pltpu.make_async_copy(hidden_far, hidden_ref, sems.at[3]),
    ]
    for copy in copies:
        copy.start()
    copies[0].wait()
    padded_ref[...] = padded(keys_ref[...])
    last = pltpu.make_async_copy(padded_ref, bank_far.at[pl.ds(ROWS, KEYS)], sems.at[4])
    last.start()
    copies[2].wait()
    copies[3].wait()
    x = hidden_ref[...]
    weighted = x.astype(f32) * (gain_ref[...] * gain_ref[...])
    hi, lo = split(weighted)
    products = dot_t(jnp.concatenate([hi, lo, x], axis=0), x)
    gram = products[:128] + products[128:256]
    up = iota((SEQ, 128), 0) < iota((SEQ, 128), 1)
    both = jnp.where(up, gram[:SEQ], pltpu.roll(gram[SEQ:], SEQ, 1))
    left = iota((32, 128), 1) < SEQ
    packed = jnp.where(left, both[:32], pltpu.roll(both[32:], SEQ, 1))
    token = diagonal(products[256:])
    diag = diagonal(gram)
    row = iota((8, 128), 0)
    sums = jnp.where(row == 0, token, jnp.where(row == 1, diag, 0.0))
    for peer in range(8):
        out_ref[peer, :32] = packed
        out_ref[peer, 32:] = sums
    copies[1].wait()
    last.wait()


def query_kernel(
    sums_ref, hidden_ref, gain_ref, pick_ref, weight_ref, positive_ref, payload_ref, query_ref, stat_ref, index_ref
):
    total = sums_ref[0]
    for peer in range(1, 8):
        total = total + sums_ref[peer]
    token = total[32:33]
    diag = total[33:34]
    inverse = lax.rsqrt(token / WIDTH + NORM_EPS)
    inverse_column = column(inverse)
    first = iota((1, 128), 1) < SEQ
    both = jnp.concatenate([total[:32], pltpu.roll(total[:32], SEQ, 1)], axis=0)
    t, u = iota((SEQ, 128), 0), iota((SEQ, 128), 1)
    second = pltpu.roll(jnp.broadcast_to(inverse, (8, 128)), SEQ, 1)[:1]
    pair = jnp.where(t < u, inverse_column[:SEQ] * inverse, inverse_column[SEQ:] * second)
    pair = jnp.where((t != u) & (u < SEQ), pair * both, 0.0)
    own = diag * inverse * inverse
    lengths = []
    for mask, on in ((first, t < u), (jnp.logical_not(first), t > u)):
        off = jnp.sum(jnp.where(on, pair, 0.0), axis=0, keepdims=True)
        square = jnp.sum(2.0 * off + jnp.where(mask, own, 0.0), axis=1, keepdims=True)
        lengths.append(jnp.sqrt(square) / SEQ)
    weighted = hidden_ref[...].astype(f32) * inverse_column
    gain = gain_ref[...]
    blocks = []
    for q in range(2):
        pooled = jnp.sum(weighted[q * SEQ:(q + 1) * SEQ], axis=0, keepdims=True) * gain / SEQ
        query = pooled / lengths[q]
        query_ref[q:q + 1] = query
        blocks.append(fold(query))
    half = jnp.concatenate(blocks, axis=0).astype(bf16)
    for z in range(16):
        payload_ref[z] = half
    length_row = jnp.where(first, lengths[0], lengths[1])
    stat_ref[...] = jnp.where(iota((8, 128), 0) == 0, inverse, length_row)
    indices = [
        pick_ref[...].astype(f32),
        weight_ref[...],
        jnp.broadcast_to(positive_ref[...].astype(f32), (8, 128)),
    ]
    index_ref[...] = own_lanes(jnp.concatenate(indices, axis=0))


def score_kernel(gathered_ref, bank_ref, out_ref, rows_ref):
    rows_ref[...] = gathered_ref[...].astype(f32).reshape(OWN * CHUNKS, 128)
    queries = jnp.concatenate(
        [rows_ref[pl.ds(c, OWN, stride=CHUNKS), :].astype(bf16) for c in range(CHUNKS)], axis=1
    )
    dots, squares = [], []
    for b in range(BANKS):
        dots.append(dot_t(bank_ref[b], queries))
        rows = bank_ref[b, :ROWS].astype(f32)
        part = rows[:, :128] * rows[:, :128]
        for c in range(1, CHUNKS):
            chunk = rows[:, c * 128:(c + 1) * 128]
            part = part + chunk * chunk
        total = jnp.sum(part, axis=1, keepdims=True)
        squares += [flat(total[:128]), flat(total[128:])]
    dots = jnp.concatenate(dots, axis=1)
    squares = jnp.concatenate(squares, axis=0)
    for peer in range(4):
        out_ref[peer, :ROWS + 8] = dots[:ROWS + 8]
        out_ref[peer, ROWS + 8:] = squares


def sum_kernel(parts_ref, out_ref):
    out_ref[...] = (parts_ref[0] + parts_ref[1]) + (parts_ref[2] + parts_ref[3])


def quantized(rows):
    most = jnp.maximum(jnp.max(jnp.abs(rows), axis=1, keepdims=True), 1e-30)
    level = jnp.floor(jnp.log(most) * FINE + 0.5) / FINE
    return whole(rows * (FULL * jnp.exp(-level))).astype(jnp.int16), level


def grad_kernel(dots_ref, index_ref, bank_ref, out_ref):
    dots = dots_ref[0] + dots_ref[1]
    queue_dots = dots[:ROWS]
    key_dots = dots[ROWS:ROWS + 8]
    z = lax.axis_index("z")
    group = iota((1, 128), 1) // OWN
    halves = []
    for half in range(2):
        wide = column(dots[ROWS + 8 + half:ROWS + 9 + half])
        for b in range(1, BANKS):
            at = ROWS + 8 + 2 * b + half
            wide = jnp.where(group == b, column(dots[at:at + 1]), wide)
        halves.append(wide)
    square = jnp.concatenate(halves, axis=0)
    index = iota((ROWS, 128), 0)
    rows = whole(index_ref[:16])
    shard = rows // ROWS
    present = (shard // 2 % 16 == z) & (shard // 32 * 2 + shard % 2 == group)
    pick = jnp.where(present, rows % ROWS, -1)
    beta = index_ref[16:32]
    target = whole(index_ref[32:33])
    shard = target // 2
    held = (shard // 2 % 16 == z) & (shard // 32 * 2 + shard % 2 == group)
    target = jnp.where(held, target % 2, -1)
    cosines, squares = [], []
    for h in range(SLOTS):
        on = index == pick[h:h + 1]
        cosines.append(jnp.sum(jnp.where(on, queue_dots, 0.0), axis=0, keepdims=True))
        squares.append(jnp.sum(jnp.where(on, square, 0.0), axis=0, keepdims=True))
    cosine = jnp.concatenate(cosines, axis=0)
    picked = jnp.concatenate(squares, axis=0)
    rest = 1.0 - beta
    numer = beta + rest * cosine
    radius_sq = beta * beta + rest * rest * picked + 2.0 * beta * rest * cosine + MIX_EPS
    radius_sq = jnp.where(present, radius_sq, 1.0)
    radius = jnp.sqrt(radius_sq)
    mixed = numer * INV_TEMP / radius
    slope = (rest - numer * beta * rest / radius_sq) * INV_TEMP / radius
    low = -1e30
    mixed = jnp.where(present, mixed, low)
    queue_scores = queue_dots * INV_TEMP
    key_row = iota((8, 128), 0)
    own = key_row == target
    positive = jnp.sum(jnp.where(own, key_dots * INV_TEMP, 0.0), axis=0, keepdims=True)
    positive = over_banks(jnp.maximum, jnp.where(held, positive, ABSENT))
    other = (key_row < 2) & jnp.logical_not(own)
    key_scores = jnp.where(other, key_dots * INV_TEMP, low)
    top = jnp.maximum(
        jnp.maximum(
            jnp.max(queue_scores, axis=0, keepdims=True), jnp.max(key_scores, axis=0, keepdims=True)
        ),
        jnp.max(mixed, axis=0, keepdims=True),
    )
    top = over_banks(jnp.maximum, top)
    queue_exp = jnp.exp(queue_scores - top)
    key_exp = jnp.where(other, jnp.exp(key_scores - top), 0.0)
    mixed_exp = jnp.where(present, jnp.exp(mixed - top), 0.0)
    mass = (
        jnp.sum(queue_exp, axis=0, keepdims=True)
        + jnp.sum(key_exp, axis=0, keepdims=True)
        + jnp.sum(mixed_exp, axis=0, keepdims=True)
    )
    mass = over_banks(jnp.add, mass)
    extra = jnp.where(present, mixed_exp * slope, 0.0)
    coef = queue_exp * INV_TEMP
    for h in range(SLOTS):
        coef = coef + jnp.where(index == pick[h:h + 1], extra[h:h + 1], 0.0)
    hi, lo = split(jnp.transpose(coef))
    blank = jnp.zeros((8, 128), f32)
    small = [key_exp * INV_TEMP, blank, jnp.where(own, 1.0, 0.0), blank, jnp.zeros((96, 128), f32)]
    small = jnp.transpose(jnp.concatenate(small, axis=0))
    key_hi, key_lo = split(small)
    chosen = pltpu.roll(small, 112, 1).astype(bf16)
    product = functools.partial(jnp.dot, preferred_element_type=f32)
    sums = jnp.zeros((2 * OWN, PART), f32)
    extras = jnp.zeros((3 * OWN, PART), f32)
    for b in range(BANKS):
        at = slice(b * OWN, (b + 1) * OWN)
        sums = sums + product(jnp.concatenate([hi[at], lo[at]], axis=0), bank_ref[b, :ROWS])
        few = jnp.concatenate([key_hi[at], key_lo[at], chosen[at]], axis=0)[:, :KEYS]
        extras = extras + product(few, bank_ref[b, ROWS:])
    sums = (sums[:OWN] + sums[OWN:]) + (extras[:OWN] + extras[OWN:2 * OWN])
    out_ref[:, :PART], level = quantized(sums)
    out_ref[:, PART:2 * PART], key_level = quantized(extras[2 * OWN:])
    lane = iota((OWN, 128), 1)
    stats = jnp.where(lane == 0, column(top)[:OWN], 0.0)
    stats = jnp.where(lane == 1, column(mass)[:OWN], stats)
    stats = jnp.where(lane == 2, column(positive)[:OWN], stats)
    stats = jnp.where(lane == 3, level, jnp.where(lane == 4, key_level, stats))
    pieces = jnp.floor(stats)
    rest = (stats - pieces) * FINE
    middle = jnp.floor(rest)
    last = jnp.floor((rest - middle) * FINE)
    middle = middle - 32768.0
    last = last - 32768.0
    block = jnp.where(lane < 8, pieces, jnp.where(lane < 16, pltpu.roll(middle, 8, 1), pltpu.roll(last, 16, 1)))
    out_ref[:, 2 * PART:] = jnp.where(lane < 24, block, 0.0).astype(jnp.int32).astype(jnp.int16)


def inner_kernel(parts_ref, query_ref, hidden_ref, gain_ref, out_ref, grad_ref):
    pieces = parts_ref[:, 2 * PART:].astype(jnp.int32).astype(f32)
    middle = pltpu.roll(pieces, 120, 1) + 32768.0
    last = pltpu.roll(pieces, 112, 1) + 32768.0
    stats = pieces + (middle + last / FINE) / FINE
    tops = stats[:, 0:1]
    positives = stats[:, 2:3]
    even = iota((OWN, 1), 0) % 2 == 0
    both = jnp.maximum(tops, positives)
    top = jnp.where(
        even,
        jnp.max(jnp.where(even, both, ABSENT), axis=0, keepdims=True),
        jnp.max(jnp.where(even, ABSENT, both), axis=0, keepdims=True),
    )
    scale = jnp.exp(tops - top)
    mass = stats[:, 1:2] * scale
    own = jnp.exp(positives - top)

    def folded(at, factor):
        rows = parts_ref[:, at:at + PART].astype(jnp.int32).astype(f32) * (factor / FULL)
        rows = (rows[:8] + rows[8:16]) + (rows[16:24] + rows[24:])
        return (rows[0:2] + rows[2:4]) + (rows[4:6] + rows[6:8])

    sums = folded(0, scale * jnp.exp(stats[:, 3:4]))
    key = folded(PART, jnp.exp(stats[:, 4:5]))
    others, full = [], []
    for mask in (even, jnp.logical_not(even)):
        others.append(jnp.sum(jnp.where(mask, mass, 0.0), axis=0, keepdims=True))
        full.append(others[-1] + jnp.sum(jnp.where(mask, own, 0.0), axis=0, keepdims=True))
    others = jnp.concatenate(others, axis=0)
    full = jnp.concatenate(full, axis=0)
    share = others / full
    sums = sums / full
    grad = LOSS_SCALE * (sums - key * (share * INV_TEMP))
    grad_ref[...] = grad
    query = query_ref[...]
    gain = gain_ref[...]
    along = jnp.sum(query * grad, axis=1, keepdims=True)
    rows = jnp.concatenate([grad * gain, query * gain, jnp.zeros((4, PART), f32)], axis=0)
    hi = rows.astype(bf16).astype(f32)
    mid = (rows - hi).astype(bf16).astype(f32)
    pieces = jnp.concatenate([hi, mid, rows - hi - mid, jnp.zeros((8, PART), f32)], axis=0).astype(bf16)
    dots = dot_t(pieces, hidden_ref[...])
    dots = dots[:8] + (dots[8:16] + dots[16:24])
    first = iota((1, 128), 1) < SEQ
    of_grad = jnp.where(first, dots[0:1], dots[1:2])
    of_query = jnp.where(first, dots[2:3], dots[3:4])
    of_along = jnp.where(first, along[0:1], along[1:2])
    row = iota((8, 128), 0)
    block = jnp.where(row == 0, of_grad, jnp.where(row == 1, of_query, of_along))
    for peer in range(8):
        out_ref[peer] = block


def output_kernel(sums_ref, grad_ref, query_ref, stat_ref, hidden_ref, gain_ref, out_ref):
    total = sums_ref[0]
    for peer in range(1, 8):
        total = total + sums_ref[peer]
    inverse = stat_ref[0:1]
    length = stat_ref[1:2]
    along = total[2:3]
    inner = inverse * (total[0:1] - along * total[1:2]) / (length * WIDTH)
    inverse_column = column(inverse)
    slide = column(inverse * inverse * inner) / SEQ
    gain = gain_ref[...]
    for q in range(2):
        at = q * SEQ
        scaled = (
            gain * (grad_ref[q:q + 1] - along[:, at:at + 1] * query_ref[q:q + 1])
            / (length[:, at:at + 1] * SEQ)
        )
        out_ref[at:at + SEQ] = (
            inverse_column[at:at + SEQ] * scaled
            - hidden_ref[at:at + SEQ].astype(f32) * slide[at:at + SEQ]
        )


def shape(dims, kind=f32):
    return jax.ShapeDtypeStruct(dims, kind)


def shards(hidden, gain, keys, queue, positive, mix_rows, mix_weight):
    tokens = hidden.reshape(TOKENS, PART)
    gain = gain.reshape(1, PART)
    squares, bank = call(
        squares_kernel, [shape((8, 40, 128)), shape((BANK, PART), bf16)], tokens, queue, gain, keys,
        far=(0, 1, 2, 3), far_outs=(1,), vmem=63 << 20,
        scratch=[
            pltpu.VMEM((TOKENS, PART), bf16),
            pltpu.VMEM((1, PART), f32),
            pltpu.VMEM((2, PART), bf16),
            pltpu.VMEM((KEYS, PART), bf16),
            pltpu.SemaphoreType.DMA((5,)),
        ],
    )
    bank = lax.all_gather(bank, ("xh", "c"))
    squares = lax.all_to_all(squares, PIPE, 0, 0)
    payload, query, stat, index = call(
        query_kernel,
        [shape((16, 16, 128), bf16), shape((2, PART)), shape((8, 128)), shape((40, 128))],
        squares, tokens, gain, mix_rows.T, mix_weight.T, positive.reshape(1, QUERIES),
    )
    gathered = lax.all_to_all(payload, "z", 0, 0)
    dots = call(
        score_kernel, shape((4, BANK, 128)), gathered, bank, scratch=[pltpu.VMEM((OWN * CHUNKS, 128), f32)]
    )
    dots = lax.all_to_all(dots, "y", 0, 0)
    dots = lax.all_gather(call(sum_kernel, shape((BANK, 128)), dots), "xl")
    parts = call(grad_kernel, shape((OWN, EXT), jnp.int16), dots, index, bank)
    parts = lax.all_to_all(parts.reshape(16, 2, EXT), "z", 0, 0).reshape(OWN, EXT)
    sums, grad = call(
        inner_kernel, [shape((8, 8, 128)), shape((2, PART))], parts, query, tokens, gain
    )
    sums = lax.all_to_all(sums, PIPE, 0, 0)
    out = call(output_kernel, shape((TOKENS, PART)), sums, grad, query, stat, tokens, gain)
    return out.reshape(2, SEQ, PART)


def solution(mesh):
    fine = Mesh(mesh.devices.reshape(2, 16, 2, 4, 2), ("xh", "z", "c", "y", "xl"))
    dp = ("xh", "z", "c")
    placed = (P(dp, None, PIPE), P(PIPE), P(dp, PIPE), P(dp, PIPE), P(), P(), P())
    return jax.shard_map(
        shards, mesh=fine, in_specs=placed, out_specs=P(dp, None, PIPE), check_vma=False
    )
```

```python
import functools

import jax
import jax.numpy as jnp
from jax import lax
from jax.experimental import pallas as pl
from jax.experimental.pallas import tpu as pltpu
from jax.sharding import Mesh, PartitionSpec as P

NORM_EPS = 1e-05
MIX_EPS = 1e-06
INV_TEMP = 20.0
LOSS_SCALE = 2048.0
WIDTH = 8192
PART = 1024
CHUNKS = 8
SEQ = 64
TOKENS = 128
QUERIES = 128
ROWS = 256
KEYS = 16
BANK = ROWS + KEYS
BANKS = 4
OWN = 32
SLOTS = 16
EXT = 2 * PART + 128
ABSENT = -30000.0
FINE = 65536.0
FULL = 32000.0
PIPE = ("y", "xl")
VMEM = 24 << 20

f32 = jnp.float32
bf16 = jnp.bfloat16


def dot_t(a, b):
    return lax.dot_general(a, b, (((1,), (1,)), ((), ())), preferred_element_type=f32)


def split(a):
    hi = a.astype(bf16)
    return hi, (a - hi.astype(f32)).astype(bf16)


def iota(shape, dim):
    return lax.broadcasted_iota(jnp.int32, shape, dim)


def padded(keys):
    return jnp.concatenate([keys.astype(f32), jnp.zeros((KEYS - 2, PART), f32)], axis=0).astype(bf16)


def own_lanes(rows):
    old, new = iota((128, 128), 0), iota((128, 128), 1) % OWN
    place = ((lax.axis_index("xh") * 16 + new // 2) * 2 + lax.axis_index("c")) * 2 + new % 2
    chosen = jnp.where(old == place, 1.0, 0.0).astype(bf16)
    hi = rows.astype(bf16)
    rest = rows - hi.astype(f32)
    mid = rest.astype(bf16)
    low = (rest - mid.astype(f32)).astype(bf16)
    product = functools.partial(jnp.dot, preferred_element_type=f32)
    return product(hi, chosen) + (product(mid, chosen) + product(low, chosen))


def spread(rows, lanes):
    hi = rows.astype(bf16).astype(f32)
    mid = (rows - hi).astype(bf16).astype(f32)
    pieces = jnp.concatenate([hi, mid, rows - hi - mid, jnp.zeros((8, 128), f32)], axis=0).astype(bf16)
    chosen = jnp.where(iota((32, 128), 0) % 8 == lanes, 1.0, 0.0).astype(bf16)
    return lax.dot_general(pieces, chosen, (((0,), (0,)), ((), ())), preferred_element_type=f32)


def over_banks(op, row):
    block = jnp.broadcast_to(row, (8, 128))
    block = op(block, pltpu.roll(block, 64, 1))
    return op(block, pltpu.roll(block, 32, 1))[:1]


def whole(a):
    return jnp.floor(a + 0.5).astype(jnp.int32)


def diagonal(square):
    n = square.shape[0]
    on = iota((n, n), 0) == iota((n, n), 1)
    return jnp.sum(jnp.where(on, square, 0.0), axis=0, keepdims=True)


def flat(tall):
    on = iota((128, 128), 0) == iota((128, 128), 1)
    return jnp.sum(jnp.where(on, tall, 0.0), axis=0, keepdims=True)


def column(row):
    on = iota((128, 128), 0) == iota((128, 128), 1)
    return jnp.sum(jnp.where(on, row, 0.0), axis=1, keepdims=True)


def fold(row):
    return jnp.concatenate([row[:, c * 128:(c + 1) * 128] for c in range(CHUNKS)], axis=0)


def unfold(block):
    return jnp.concatenate([block[c:c + 1] for c in range(CHUNKS)], axis=1)


def call(kernel, outs, *args, far=(), far_outs=(), scratch=(), vmem=VMEM):
    def place(i, far):
        return pl.BlockSpec(memory_space=pltpu.HBM if i in far else pltpu.VMEM)

    many = isinstance(outs, (list, tuple))
    return pl.pallas_call(
        kernel,
        out_shape=outs,
        in_specs=[place(i, far) for i in range(len(args))],
        out_specs=[place(i, far_outs) for i in range(len(outs))] if many else place(0, far_outs),
        scratch_shapes=scratch,
        compiler_params=pltpu.CompilerParams(vmem_limit_bytes=vmem),
    )(*args)


def squares_kernel(
    hidden_far, queue_far, gain_far, keys_far, out_ref, bank_ref, hidden_ref, gain_ref, keys_ref, sems
):
    copies = [
        pltpu.make_async_copy(source, target, sems.at[i])
        for i, (source, target) in enumerate((
            (keys_far, keys_ref),
            (gain_far, gain_ref),
            (hidden_far, hidden_ref),
            (queue_far, bank_ref.at[pl.ds(0, ROWS)]),
        ))
    ]
    for copy in copies:
        copy.start()
    for copy in copies[:-1]:
        copy.wait()
    bank_ref[ROWS:] = padded(keys_ref[...])
    x = hidden_ref[...]
    weighted = x.astype(f32) * (gain_ref[...] * gain_ref[...])
    hi, lo = split(weighted)
    products = dot_t(jnp.concatenate([hi, lo, x], axis=0), x)
    gram = products[:128] + products[128:256]
    up = iota((SEQ, 128), 0) < iota((SEQ, 128), 1)
    both = jnp.where(up, gram[:SEQ], pltpu.roll(gram[SEQ:], SEQ, 1))
    left = iota((32, 128), 1) < SEQ
    packed = jnp.where(left, both[:32], pltpu.roll(both[32:], SEQ, 1))
    token = diagonal(products[256:])
    diag = diagonal(gram)
    row = iota((8, 128), 0)
    sums = jnp.where(row == 0, token, jnp.where(row == 1, diag, 0.0))
    for peer in range(8):
        out_ref[peer, :32] = packed
        out_ref[peer, 32:] = sums
    copies[-1].wait()


def query_kernel(sums_ref, hidden_ref, gain_ref, payload_ref, query_ref, stat_ref):
    total = sums_ref[0]
    for peer in range(1, 8):
        total = total + sums_ref[peer]
    token = total[32:33]
    diag = total[33:34]
    inverse = lax.rsqrt(token / WIDTH + NORM_EPS)
    inverse_column = column(inverse)
    first = iota((1, 128), 1) < SEQ
    both = jnp.concatenate([total[:32], pltpu.roll(total[:32], SEQ, 1)], axis=0)
    t, u = iota((SEQ, 128), 0), iota((SEQ, 128), 1)
    second = pltpu.roll(jnp.broadcast_to(inverse, (8, 128)), SEQ, 1)[:1]
    pair = jnp.where(t < u, inverse_column[:SEQ] * inverse, inverse_column[SEQ:] * second)
    pair = jnp.where((t != u) & (u < SEQ), pair * both, 0.0)
    own = diag * inverse * inverse
    lengths = []
    for mask, on in ((first, t < u), (jnp.logical_not(first), t > u)):
        off = jnp.sum(jnp.where(on, pair, 0.0), axis=0, keepdims=True)
        square = jnp.sum(2.0 * off + jnp.where(mask, own, 0.0), axis=1, keepdims=True)
        lengths.append(jnp.sqrt(square) / SEQ)
    weighted = hidden_ref[...].astype(f32) * inverse_column
    gain = gain_ref[...]
    blocks = []
    for q in range(2):
        pooled = jnp.sum(weighted[q * SEQ:(q + 1) * SEQ], axis=0, keepdims=True) * gain / SEQ
        query = pooled / lengths[q]
        query_ref[q:q + 1] = query
        blocks.append(fold(query))
    half = jnp.concatenate(blocks, axis=0).astype(bf16)
    for z in range(16):
        payload_ref[z] = half
    length_row = jnp.where(first, lengths[0], lengths[1])
    stat_ref[...] = jnp.where(iota((8, 128), 0) == 0, inverse, length_row)


def pair_kernel(own_ref, came_ref, after_ref, out_ref):
    del after_ref
    out_ref[0] = own_ref[...]
    out_ref[1] = came_ref[...]


def bank_dots(bank_ref, queries):
    dots, squares = [], []
    for b in range(2):
        dots.append(dot_t(bank_ref[b], queries))
        rows = bank_ref[b, :ROWS].astype(f32)
        part = rows[:, :128] * rows[:, :128]
        for c in range(1, CHUNKS):
            chunk = rows[:, c * 128:(c + 1) * 128]
            part = part + chunk * chunk
        total = jnp.sum(part, axis=1, keepdims=True)
        squares += [flat(total[:128]), flat(total[128:])]
    return dots, squares


def near_kernel(
    gathered_ref, near_ref, pick_ref, weight_ref, positive_ref, out_ref, queries_ref, index_ref, rows_ref
):
    indices = [
        pick_ref[...].astype(f32),
        weight_ref[...],
        jnp.broadcast_to(positive_ref[...].astype(f32), (8, 128)),
    ]
    index_ref[...] = own_lanes(jnp.concatenate(indices, axis=0))
    rows_ref[...] = gathered_ref[...].astype(f32).reshape(OWN * CHUNKS, 128)
    queries = jnp.concatenate(
        [rows_ref[pl.ds(c, OWN, stride=CHUNKS), :].astype(bf16) for c in range(CHUNKS)], axis=1
    )
    queries_ref[...] = queries
    dots, squares = bank_dots(near_ref, queries)
    out_ref[:ROWS + 8] = jnp.concatenate([d[:ROWS + 8] for d in dots] * 2, axis=1)
    out_ref[ROWS + 8:] = jnp.concatenate(squares * 2, axis=0)


def far_kernel(part_ref, queries_ref, far_ref, out_ref):
    dots, squares = bank_dots(far_ref, queries_ref[...])
    dots = jnp.concatenate([d[:ROWS + 8] for d in dots] * 2, axis=1)
    dots = jnp.where(iota((ROWS + 8, 128), 1) < 2 * OWN, part_ref[:ROWS + 8], dots)
    squares = jnp.concatenate([part_ref[ROWS + 8:ROWS + 12]] + squares, axis=0)
    for peer in range(4):
        out_ref[peer, :ROWS + 8] = dots
        out_ref[peer, ROWS + 8:] = squares


def sum_kernel(parts_ref, out_ref):
    out_ref[...] = (parts_ref[0] + parts_ref[1]) + (parts_ref[2] + parts_ref[3])


def quantized(rows):
    most = jnp.maximum(jnp.max(jnp.abs(rows), axis=1, keepdims=True), 1e-30)
    level = jnp.floor(jnp.log(most) * FINE + 0.5) / FINE
    return whole(rows * (FULL * jnp.exp(-level))).astype(jnp.int16), level


def bank_of(shard):
    across = (shard // 32 != lax.axis_index("xh")).astype(jnp.int32)
    beside = (shard % 2 != lax.axis_index("c")).astype(jnp.int32)
    return jnp.where(shard // 2 % 16 == lax.axis_index("z"), across + 2 * beside, -1)


def grad_kernel(dots_ref, index_ref, near_ref, far_ref, out_ref):
    dots = dots_ref[0] + dots_ref[1]
    queue_dots = dots[:ROWS]
    key_dots = dots[ROWS:ROWS + 8]
    group = iota((1, 128), 1) // OWN
    square = jnp.concatenate([spread(dots[ROWS + 8:], 2 * group + half) for half in range(2)], axis=0)
    index = iota((ROWS, 128), 0)
    rows = whole(index_ref[:16])
    present = bank_of(rows // ROWS) == group
    pick = jnp.where(present, rows % ROWS, -8)
    beta = index_ref[16:32]
    target = whole(index_ref[32:33])
    held = bank_of(target // 2) == group
    target = jnp.where(held, target % 2, -1)
    tile, inside = pick // 8, pick % 8
    sublane = iota((8, 128), 0)
    cosines, squares = [], []
    for h in range(SLOTS):
        chosen = jnp.zeros((8, 128), f32)
        scale = jnp.zeros((8, 128), f32)
        for t in range(ROWS // 8):
            on = tile[h:h + 1] == t
            chosen = jnp.where(on, queue_dots[8 * t:8 * t + 8], chosen)
            scale = jnp.where(on, square[8 * t:8 * t + 8], scale)
        here = sublane == inside[h:h + 1]
        cosines.append(jnp.sum(jnp.where(here, chosen, 0.0), axis=0, keepdims=True))
        squares.append(jnp.sum(jnp.where(here, scale, 0.0), axis=0, keepdims=True))
    cosine = jnp.concatenate(cosines, axis=0)
    picked = jnp.concatenate(squares, axis=0)
    rest = 1.0 - beta
    numer = beta + rest * cosine
    radius_sq = beta * beta + rest * rest * picked + 2.0 * beta * rest * cosine + MIX_EPS
    radius_sq = jnp.where(present, radius_sq, 1.0)
    radius = jnp.sqrt(radius_sq)
    mixed = numer * INV_TEMP / radius
    slope = (rest - numer * beta * rest / radius_sq) * INV_TEMP / radius
    low = -1e30
    mixed = jnp.where(present, mixed, low)
    queue_scores = queue_dots * INV_TEMP
    key_row = iota((8, 128), 0)
    own = key_row == target
    positive = jnp.sum(jnp.where(own, key_dots * INV_TEMP, 0.0), axis=0, keepdims=True)
    positive = over_banks(jnp.maximum, jnp.where(held, positive, ABSENT))
    other = (key_row < 2) & jnp.logical_not(own)
    key_scores = jnp.where(other, key_dots * INV_TEMP, low)
    top = jnp.maximum(
        jnp.maximum(
            jnp.max(queue_scores, axis=0, keepdims=True), jnp.max(key_scores, axis=0, keepdims=True)
        ),
        jnp.max(mixed, axis=0, keepdims=True),
    )
    top = over_banks(jnp.maximum, top)
    queue_exp = jnp.exp(queue_scores - top)
    key_exp = jnp.where(other, jnp.exp(key_scores - top), 0.0)
    mixed_exp = jnp.where(present, jnp.exp(mixed - top), 0.0)
    mass = (
        jnp.sum(queue_exp, axis=0, keepdims=True)
        + jnp.sum(key_exp, axis=0, keepdims=True)
        + jnp.sum(mixed_exp, axis=0, keepdims=True)
    )
    mass = over_banks(jnp.add, mass)
    extra = jnp.where(present, mixed_exp * slope, 0.0)
    coef = queue_exp * INV_TEMP
    for h in range(SLOTS):
        coef = coef + jnp.where(index == pick[h:h + 1], extra[h:h + 1], 0.0)
    hi, lo = split(jnp.transpose(coef))
    blank = jnp.zeros((8, 128), f32)
    small = [key_exp * INV_TEMP, blank, jnp.where(own, 1.0, 0.0), blank, jnp.zeros((96, 128), f32)]
    small = jnp.transpose(jnp.concatenate(small, axis=0))
    lane = iota((OWN, 128), 1)
    product = functools.partial(jnp.dot, preferred_element_type=f32)
    sums = jnp.zeros((2 * OWN, PART), f32)
    few = jnp.zeros((OWN, 128), f32)
    keys = []
    for b in range(BANKS):
        at = slice(b * OWN, (b + 1) * OWN)
        bank_ref = (near_ref, far_ref)[b // 2]
        sums = sums + product(jnp.concatenate([hi[at], lo[at]], axis=0), bank_ref[b % 2, :ROWS])
        few = jnp.where(lane % KEYS // 2 == b, pltpu.roll(small[at], 2 * b, 1), few)
        keys.append(bank_ref[b % 2, ROWS:].astype(f32)[:2])
    keys = jnp.concatenate(keys + [jnp.zeros((KEYS - 8, PART), f32)], axis=0).astype(bf16)
    chosen = pltpu.roll(few, 128 - KEYS, 1)
    few_hi = few.astype(bf16).astype(f32)
    few = jnp.concatenate([few_hi, few - few_hi, chosen], axis=0).astype(bf16)[:, :KEYS]
    extras = product(few, keys)
    sums = (sums[:OWN] + sums[OWN:]) + (extras[:OWN] + extras[OWN:2 * OWN])
    out_ref[:, :PART], level = quantized(sums)
    out_ref[:, PART:2 * PART], key_level = quantized(extras[2 * OWN:])
    rows = jnp.concatenate([top, mass, positive, jnp.zeros((5, 128), f32)], axis=0)
    stats = spread(rows, jnp.where(iota((1, 128), 1) < 3, iota((1, 128), 1), -1))[:OWN]
    stats = jnp.where(lane == 3, level, jnp.where(lane == 4, key_level, stats))
    pieces = jnp.floor(stats)
    rest = (stats - pieces) * FINE
    middle = jnp.floor(rest)
    last = jnp.floor((rest - middle) * FINE)
    middle = middle - 32768.0
    last = last - 32768.0
    block = jnp.where(lane < 8, pieces, jnp.where(lane < 16, pltpu.roll(middle, 8, 1), pltpu.roll(last, 16, 1)))
    out_ref[:, 2 * PART:] = jnp.where(lane < 24, block, 0.0).astype(jnp.int32).astype(jnp.int16)


def inner_kernel(parts_ref, query_ref, hidden_ref, gain_ref, out_ref, grad_ref):
    pieces = parts_ref[:, 2 * PART:].astype(jnp.int32).astype(f32)
    middle = pltpu.roll(pieces, 120, 1) + 32768.0
    last = pltpu.roll(pieces, 112, 1) + 32768.0
    stats = pieces + (middle + last / FINE) / FINE
    tops = stats[:, 0:1]
    positives = stats[:, 2:3]
    even = iota((OWN, 1), 0) % 2 == 0
    both = jnp.maximum(tops, positives)
    top = jnp.where(
        even,
        jnp.max(jnp.where(even, both, ABSENT), axis=0, keepdims=True),
        jnp.max(jnp.where(even, ABSENT, both), axis=0, keepdims=True),
    )
    scale = jnp.exp(tops - top)
    mass = stats[:, 1:2] * scale
    own = jnp.exp(positives - top)

    def folded(at, factor):
        rows = parts_ref[:, at:at + PART].astype(jnp.int32).astype(f32) * (factor / FULL)
        rows = (rows[:8] + rows[8:16]) + (rows[16:24] + rows[24:])
        return (rows[0:2] + rows[2:4]) + (rows[4:6] + rows[6:8])

    sums = folded(0, scale * jnp.exp(stats[:, 3:4]))
    key = folded(PART, jnp.exp(stats[:, 4:5]))
    others, full = [], []
    for mask in (even, jnp.logical_not(even)):
        others.append(jnp.sum(jnp.where(mask, mass, 0.0), axis=0, keepdims=True))
        full.append(others[-1] + jnp.sum(jnp.where(mask, own, 0.0), axis=0, keepdims=True))
    others = jnp.concatenate(others, axis=0)
    full = jnp.concatenate(full, axis=0)
    share = others / full
    sums = sums / full
    grad = LOSS_SCALE * (sums - key * (share * INV_TEMP))
    grad_ref[...] = grad
    query = query_ref[...]
    gain = gain_ref[...]
    along = jnp.sum(query * grad, axis=1, keepdims=True)
    rows = jnp.concatenate([grad * gain, query * gain, jnp.zeros((4, PART), f32)], axis=0)
    hi = rows.astype(bf16).astype(f32)
    mid = (rows - hi).astype(bf16).astype(f32)
    pieces = jnp.concatenate([hi, mid, rows - hi - mid, jnp.zeros((8, PART), f32)], axis=0).astype(bf16)
    dots = dot_t(pieces, hidden_ref[...])
    dots = dots[:8] + (dots[8:16] + dots[16:24])
    first = iota((1, 128), 1) < SEQ
    of_grad = jnp.where(first, dots[0:1], dots[1:2])
    of_query = jnp.where(first, dots[2:3], dots[3:4])
    of_along = jnp.where(first, along[0:1], along[1:2])
    row = iota((8, 128), 0)
    block = jnp.where(row == 0, of_grad, jnp.where(row == 1, of_query, of_along))
    for peer in range(8):
        out_ref[peer] = block


def output_kernel(sums_ref, grad_ref, query_ref, stat_ref, hidden_ref, gain_ref, out_far, out_ref, sems):
    total = sums_ref[0]
    for peer in range(1, 8):
        total = total + sums_ref[peer]
    inverse = stat_ref[0:1]
    length = stat_ref[1:2]
    along = total[2:3]
    inner = inverse * (total[0:1] - along * total[1:2]) / (length * WIDTH)
    inverse_column = column(inverse)
    slide = column(inverse * inverse * inner) / SEQ
    gain = gain_ref[...]
    copies = []
    for q in range(2):
        at = q * SEQ
        scaled = (
            gain * (grad_ref[q:q + 1] - along[:, at:at + 1] * query_ref[q:q + 1])
            / (length[:, at:at + 1] * SEQ)
        )
        out_ref[at:at + SEQ] = (
            inverse_column[at:at + SEQ] * scaled
            - hidden_ref[at:at + SEQ].astype(f32) * slide[at:at + SEQ]
        )
        part = pl.ds(at, SEQ)
        copies.append(pltpu.make_async_copy(out_ref.at[part], out_far.at[part], sems.at[q]))
        copies[-1].start()
    for copy in copies:
        copy.wait()


def shape(dims, kind=f32):
    return jax.ShapeDtypeStruct(dims, kind)


def shards(hidden, gain, keys, queue, positive, mix_rows, mix_weight):
    tokens = hidden.reshape(TOKENS, PART)
    gain = gain.reshape(1, PART)
    squares, bank = call(
        squares_kernel, [shape((8, 40, 128)), shape((BANK, PART), bf16)], tokens, queue, gain, keys,
        far=range(4), vmem=63 << 20,
        scratch=[
            pltpu.VMEM((TOKENS, PART), bf16),
            pltpu.VMEM((1, PART), f32),
            pltpu.VMEM((2, PART), bf16),
            pltpu.SemaphoreType.DMA((4,)),
        ],
    )
    swap = [(0, 1), (1, 0)]
    squares = lax.all_to_all(squares, PIPE, 0, 0)
    own, squares = lax.optimization_barrier((bank, squares))
    came = lax.ppermute(own, "xh", swap)
    payload, query, stat = call(
        query_kernel, [shape((16, 16, 128), bf16), shape((2, PART)), shape((8, 128))], squares, tokens, gain
    )
    gathered = lax.all_to_all(payload, "z", 0, 0)
    near = call(pair_kernel, shape((2, BANK, PART), bf16), own, came, gathered)
    far = lax.ppermute(near, "c", swap)
    dots, queries, index = call(
        near_kernel, [shape((BANK, 128)), shape((OWN, PART), bf16), shape((40, 128))],
        gathered, near, mix_rows.T, mix_weight.T, positive.reshape(1, QUERIES),
        scratch=[pltpu.VMEM((OWN * CHUNKS, 128), f32)],
    )
    dots = call(far_kernel, shape((4, BANK, 128)), dots, queries, far)
    dots = lax.all_to_all(dots, "y", 0, 0)
    dots = lax.all_gather(call(sum_kernel, shape((BANK, 128)), dots), "xl")
    parts = call(grad_kernel, shape((OWN, EXT), jnp.int16), dots, index, near, far)
    parts = lax.all_to_all(parts.reshape(16, 2, EXT), "z", 0, 0).reshape(OWN, EXT)
    sums, grad = call(
        inner_kernel, [shape((8, 8, 128)), shape((2, PART))], parts, query, tokens, gain
    )
    sums = lax.all_to_all(sums, PIPE, 0, 0)
    out = call(
        output_kernel, shape((TOKENS, PART)), sums, grad, query, stat, tokens, gain, far_outs=(0,),
        scratch=[pltpu.VMEM((TOKENS, PART), f32), pltpu.SemaphoreType.DMA((2,))],
    )
    return out.reshape(2, SEQ, PART)


def solution(mesh):
    fine = Mesh(mesh.devices.reshape(2, 16, 2, 4, 2), ("xh", "z", "c", "y", "xl"))
    dp = ("xh", "z", "c")
    placed = (P(dp, None, PIPE), P(PIPE), P(dp, PIPE), P(dp, PIPE), P(), P(), P())
    return jax.shard_map(
        shards, mesh=fine, in_specs=placed, out_specs=P(dp, None, PIPE), check_vma=False
    )
```

```python
import functools
import math

import jax
import jax.numpy as jnp
from jax import lax
from jax.experimental import pallas as pl
from jax.experimental.pallas import tpu as pltpu
from jax.sharding import Mesh, PartitionSpec as P

NORM_EPS = 1e-05
MIX_EPS = 1e-06
INV_TEMP = 20.0
LOSS_SCALE = 2048.0
WIDTH = 8192
PART = 1024
CHUNKS = 8
SEQ = 64
TOKENS = 128
QUERIES = 128
ROWS = 256
KEYS = 16
BANK = ROWS + KEYS
BANKS = 4
OWN = 32
SLOTS = 16
EXT = 2 * PART + 128
ABSENT = -30000.0
FINE = 65536.0
FULL = 32000.0
SENT = ROWS + 48
MOST = 0.5
PIPE = ("y", "xl")
VMEM = 24 << 20

f32 = jnp.float32
bf16 = jnp.bfloat16


def dot_t(a, b):
    return lax.dot_general(a, b, (((1,), (1,)), ((), ())), preferred_element_type=f32)


def split(a):
    hi = a.astype(bf16)
    return hi, (a - hi.astype(f32)).astype(bf16)


def iota(shape, dim):
    return lax.broadcasted_iota(jnp.int32, shape, dim)


def padded(keys):
    return jnp.concatenate([keys.astype(f32), jnp.zeros((KEYS - 2, PART), f32)], axis=0).astype(bf16)


def own_lanes(rows):
    old, new = iota((128, 128), 0), iota((128, 128), 1) % OWN
    place = ((lax.axis_index("xh") * 16 + new // 2) * 2 + lax.axis_index("c")) * 2 + new % 2
    chosen = jnp.where(old == place, 1.0, 0.0).astype(bf16)
    hi = rows.astype(bf16)
    rest = rows - hi.astype(f32)
    mid = rest.astype(bf16)
    low = (rest - mid.astype(f32)).astype(bf16)
    product = functools.partial(jnp.dot, preferred_element_type=f32)
    return product(hi, chosen) + (product(mid, chosen) + product(low, chosen))


def spread(rows, lanes):
    hi = rows.astype(bf16).astype(f32)
    mid = (rows - hi).astype(bf16).astype(f32)
    pieces = jnp.concatenate([hi, mid, rows - hi - mid, jnp.zeros((8, 128), f32)], axis=0).astype(bf16)
    chosen = jnp.where(iota((32, 128), 0) % 8 == lanes, 1.0, 0.0).astype(bf16)
    return lax.dot_general(pieces, chosen, (((0,), (0,)), ((), ())), preferred_element_type=f32)


def over_banks(op, row):
    block = jnp.broadcast_to(row, (8, 128))
    block = op(block, pltpu.roll(block, 64, 1))
    return op(block, pltpu.roll(block, 32, 1))[:1]


def whole(a):
    return jnp.floor(a + 0.5).astype(jnp.int32)


def diagonal(square):
    n = square.shape[0]
    on = iota((n, n), 0) == iota((n, n), 1)
    return jnp.sum(jnp.where(on, square, 0.0), axis=0, keepdims=True)


def flat(tall):
    on = iota((128, 128), 0) == iota((128, 128), 1)
    return jnp.sum(jnp.where(on, tall, 0.0), axis=0, keepdims=True)


def column(row):
    on = iota((128, 128), 0) == iota((128, 128), 1)
    return jnp.sum(jnp.where(on, row, 0.0), axis=1, keepdims=True)


def fold(row):
    return jnp.concatenate([row[:, c * 128:(c + 1) * 128] for c in range(CHUNKS)], axis=0)


def unfold(block):
    return jnp.concatenate([block[c:c + 1] for c in range(CHUNKS)], axis=1)


def call(kernel, outs, *args, far=(), far_outs=(), scratch=(), vmem=VMEM):
    def place(i, far):
        return pl.BlockSpec(memory_space=pltpu.HBM if i in far else pltpu.VMEM)

    many = isinstance(outs, (list, tuple))
    return pl.pallas_call(
        kernel,
        out_shape=outs,
        in_specs=[place(i, far) for i in range(len(args))],
        out_specs=[place(i, far_outs) for i in range(len(outs))] if many else place(0, far_outs),
        scratch_shapes=scratch,
        compiler_params=pltpu.CompilerParams(vmem_limit_bytes=vmem),
    )(*args)


def squares_kernel(
    hidden_far, queue_far, gain_far, keys_far, out_ref, bank_ref, hidden_ref, gain_ref, keys_ref, sems
):
    copies = [
        pltpu.make_async_copy(source, target, sems.at[i])
        for i, (source, target) in enumerate((
            (keys_far, keys_ref),
            (gain_far, gain_ref),
            (hidden_far, hidden_ref),
            (queue_far, bank_ref.at[pl.ds(0, ROWS)]),
        ))
    ]
    for copy in copies:
        copy.start()
    for copy in copies[:-1]:
        copy.wait()
    bank_ref[ROWS:] = padded(keys_ref[...])
    x = hidden_ref[...]
    weighted = x.astype(f32) * (gain_ref[...] * gain_ref[...])
    hi, lo = split(weighted)
    products = dot_t(jnp.concatenate([hi, lo, x], axis=0), x)
    gram = products[:128] + products[128:256]
    up = iota((SEQ, 128), 0) < iota((SEQ, 128), 1)
    both = jnp.where(up, gram[:SEQ], pltpu.roll(gram[SEQ:], SEQ, 1))
    left = iota((32, 128), 1) < SEQ
    packed = jnp.where(left, both[:32], pltpu.roll(both[32:], SEQ, 1))
    token = diagonal(products[256:])
    diag = diagonal(gram)
    row = iota((8, 128), 0)
    sums = jnp.where(row == 0, token, jnp.where(row == 1, diag, 0.0))
    for peer in range(8):
        out_ref[peer, :32] = packed
        out_ref[peer, 32:] = sums
    copies[-1].wait()


def query_kernel(sums_ref, hidden_ref, gain_ref, payload_ref, query_ref, stat_ref):
    total = sums_ref[0]
    for peer in range(1, 8):
        total = total + sums_ref[peer]
    token = total[32:33]
    diag = total[33:34]
    inverse = lax.rsqrt(token / WIDTH + NORM_EPS)
    inverse_column = column(inverse)
    first = iota((1, 128), 1) < SEQ
    both = jnp.concatenate([total[:32], pltpu.roll(total[:32], SEQ, 1)], axis=0)
    t, u = iota((SEQ, 128), 0), iota((SEQ, 128), 1)
    second = pltpu.roll(jnp.broadcast_to(inverse, (8, 128)), SEQ, 1)[:1]
    pair = jnp.where(t < u, inverse_column[:SEQ] * inverse, inverse_column[SEQ:] * second)
    pair = jnp.where((t != u) & (u < SEQ), pair * both, 0.0)
    own = diag * inverse * inverse
    lengths = []
    for mask, on in ((first, t < u), (jnp.logical_not(first), t > u)):
        off = jnp.sum(jnp.where(on, pair, 0.0), axis=0, keepdims=True)
        square = jnp.sum(2.0 * off + jnp.where(mask, own, 0.0), axis=1, keepdims=True)
        lengths.append(jnp.sqrt(square) / SEQ)
    weighted = hidden_ref[...].astype(f32) * inverse_column
    gain = gain_ref[...]
    blocks = []
    for q in range(2):
        pooled = jnp.sum(weighted[q * SEQ:(q + 1) * SEQ], axis=0, keepdims=True) * gain / SEQ
        query = pooled / lengths[q]
        query_ref[q:q + 1] = query
        blocks.append(fold(query))
    half = jnp.concatenate(blocks, axis=0).astype(bf16)
    for z in range(16):
        payload_ref[z] = half
    length_row = jnp.where(first, lengths[0], lengths[1])
    stat_ref[...] = jnp.where(iota((8, 128), 0) == 0, inverse, length_row)


def pair_kernel(own_ref, came_ref, after_ref, out_ref):
    del after_ref
    out_ref[0] = own_ref[...]
    out_ref[1] = came_ref[...]


def bank_dots(bank_ref, queries):
    dots, squares = [], []
    for b in range(2):
        dots.append(dot_t(bank_ref[b], queries))
        rows = bank_ref[b, :ROWS].astype(f32)
        part = rows[:, :128] * rows[:, :128]
        for c in range(1, CHUNKS):
            chunk = rows[:, c * 128:(c + 1) * 128]
            part = part + chunk * chunk
        total = jnp.sum(part, axis=1, keepdims=True)
        squares += [flat(total[:128]), flat(total[128:])]
    return dots, squares


def near_kernel(
    gathered_ref, near_ref, pick_ref, weight_ref, positive_ref, out_ref, queries_ref, index_ref, rows_ref
):
    indices = [
        pick_ref[...].astype(f32),
        weight_ref[...],
        jnp.broadcast_to(positive_ref[...].astype(f32), (8, 128)),
    ]
    index_ref[...] = own_lanes(jnp.concatenate(indices, axis=0))
    rows_ref[...] = gathered_ref[...].astype(f32).reshape(OWN * CHUNKS, 128)
    queries = jnp.concatenate(
        [rows_ref[pl.ds(c, OWN, stride=CHUNKS), :].astype(bf16) for c in range(CHUNKS)], axis=1
    )
    queries_ref[...] = queries
    dots, squares = bank_dots(near_ref, queries)
    out_ref[:ROWS + 8] = jnp.concatenate([d[:ROWS + 8] for d in dots] * 2, axis=1)
    out_ref[ROWS + 8:] = jnp.concatenate(squares * 2, axis=0)


def pieces_of(values):
    whole_part = jnp.floor(values)
    rest = (values - whole_part) * FINE
    middle = jnp.floor(rest)
    last = jnp.floor((rest - middle) * FINE)
    return whole_part, middle - 32768.0, last - 32768.0


def value_of(whole_part, middle, last):
    return whole_part + (middle + 32768.0 + (last + 32768.0) / FINE) / FINE


def far_kernel(part_ref, queries_ref, far_ref, out_ref, exact_ref):
    dots, squares = bank_dots(far_ref, queries_ref[...])
    dots = jnp.concatenate([d[:ROWS + 8] for d in dots] * 2, axis=1)
    dots = jnp.where(iota((ROWS + 8, 128), 1) < 2 * OWN, part_ref[:ROWS + 8], dots)
    squares = jnp.concatenate([part_ref[ROWS + 8:ROWS + 12]] + squares, axis=0)
    exact_ref[:ROWS + 8] = dots
    exact_ref[ROWS + 8:] = squares
    most = jnp.maximum(jnp.max(jnp.abs(dots), axis=0, keepdims=True), 1e-30)
    level = jnp.floor(jnp.log(most) * FINE + 0.5) / FINE
    coded = jnp.floor(dots * (FULL * jnp.exp(-level)) + 0.5)
    scale = jnp.concatenate(list(pieces_of(level)) + [jnp.zeros((13, 128), f32)], axis=0)
    tail = jnp.concatenate([coded[ROWS:]] + list(pieces_of(squares)) + [scale], axis=0)
    coded = coded[:ROWS].astype(jnp.int32).astype(jnp.int16)
    tail = tail.astype(jnp.int32).astype(jnp.int16)
    for peer in range(8):
        out_ref[peer, :ROWS] = coded
        out_ref[peer, ROWS:] = tail


def levels_of(coded_ref):
    levels = []
    for peer in range(8):
        tail = coded_ref[peer, ROWS:].astype(jnp.int32).astype(f32)
        levels.append(value_of(tail[32:33], tail[33:34], tail[34:35]))
    return levels, jnp.max(functools.reduce(jnp.maximum, levels), axis=1, keepdims=True) > math.log(MOST)


def decoded(coded_ref):
    levels, over = levels_of(coded_ref)
    queue_dots = jnp.zeros((ROWS, 128), f32)
    rest = jnp.zeros((16, 128), f32)
    for peer in range(8):
        tail = coded_ref[peer, ROWS:].astype(jnp.int32).astype(f32)
        factor = jnp.exp(levels[peer]) / FULL
        queue_dots = queue_dots + coded_ref[peer, :ROWS].astype(jnp.int32).astype(f32) * factor
        squares = value_of(tail[8:16], tail[16:24], tail[24:32])
        rest = rest + jnp.concatenate([tail[:8] * factor, squares], axis=0)
    return jnp.concatenate([queue_dots, rest], axis=0), over


def quantized(rows):
    most = jnp.maximum(jnp.max(jnp.abs(rows), axis=1, keepdims=True), 1e-30)
    level = jnp.floor(jnp.log(most) * FINE + 0.5) / FINE
    return whole(rows * (FULL * jnp.exp(-level))).astype(jnp.int16), level


def bank_of(shard):
    across = (shard // 32 != lax.axis_index("xh")).astype(jnp.int32)
    beside = (shard % 2 != lax.axis_index("c")).astype(jnp.int32)
    return jnp.where(shard // 2 % 16 == lax.axis_index("z"), across + 2 * beside, -1)


def coded_grad_kernel(coded_ref, index_ref, near_ref, far_ref, out_ref):
    dots, over = decoded(coded_ref)
    grad_parts(dots, jnp.where(over, 1.0, 0.0), index_ref, near_ref, far_ref, out_ref)


def exact_grad_kernel(dots_ref, index_ref, near_ref, far_ref, out_ref):
    grad_parts(dots_ref[...], jnp.zeros((1, 1), f32), index_ref, near_ref, far_ref, out_ref)


def grad_parts(dots, over, index_ref, near_ref, far_ref, out_ref):
    queue_dots = dots[:ROWS]
    key_dots = dots[ROWS:ROWS + 8]
    group = iota((1, 128), 1) // OWN
    square = jnp.concatenate([spread(dots[ROWS + 8:], 2 * group + half) for half in range(2)], axis=0)
    index = iota((ROWS, 128), 0)
    rows = whole(index_ref[:16])
    present = bank_of(rows // ROWS) == group
    pick = jnp.where(present, rows % ROWS, -8)
    beta = index_ref[16:32]
    target = whole(index_ref[32:33])
    held = bank_of(target // 2) == group
    target = jnp.where(held, target % 2, -1)
    tile, inside = pick // 8, pick % 8
    sublane = iota((8, 128), 0)
    cosines, squares = [], []
    for h in range(SLOTS):
        chosen = jnp.zeros((8, 128), f32)
        scale = jnp.zeros((8, 128), f32)
        for t in range(ROWS // 8):
            on = tile[h:h + 1] == t
            chosen = jnp.where(on, queue_dots[8 * t:8 * t + 8], chosen)
            scale = jnp.where(on, square[8 * t:8 * t + 8], scale)
        here = sublane == inside[h:h + 1]
        cosines.append(jnp.sum(jnp.where(here, chosen, 0.0), axis=0, keepdims=True))
        squares.append(jnp.sum(jnp.where(here, scale, 0.0), axis=0, keepdims=True))
    cosine = jnp.concatenate(cosines, axis=0)
    picked = jnp.concatenate(squares, axis=0)
    rest = 1.0 - beta
    numer = beta + rest * cosine
    radius_sq = beta * beta + rest * rest * picked + 2.0 * beta * rest * cosine + MIX_EPS
    radius_sq = jnp.where(present, radius_sq, 1.0)
    radius = jnp.sqrt(radius_sq)
    mixed = numer * INV_TEMP / radius
    slope = (rest - numer * beta * rest / radius_sq) * INV_TEMP / radius
    low = -1e30
    mixed = jnp.where(present, mixed, low)
    queue_scores = queue_dots * INV_TEMP
    key_row = iota((8, 128), 0)
    own = key_row == target
    positive = jnp.sum(jnp.where(own, key_dots * INV_TEMP, 0.0), axis=0, keepdims=True)
    positive = over_banks(jnp.maximum, jnp.where(held, positive, ABSENT))
    other = (key_row < 2) & jnp.logical_not(own)
    key_scores = jnp.where(other, key_dots * INV_TEMP, low)
    top = jnp.maximum(
        jnp.maximum(
            jnp.max(queue_scores, axis=0, keepdims=True), jnp.max(key_scores, axis=0, keepdims=True)
        ),
        jnp.max(mixed, axis=0, keepdims=True),
    )
    top = over_banks(jnp.maximum, top)
    queue_exp = jnp.exp(queue_scores - top)
    key_exp = jnp.where(other, jnp.exp(key_scores - top), 0.0)
    mixed_exp = jnp.where(present, jnp.exp(mixed - top), 0.0)
    mass = (
        jnp.sum(queue_exp, axis=0, keepdims=True)
        + jnp.sum(key_exp, axis=0, keepdims=True)
        + jnp.sum(mixed_exp, axis=0, keepdims=True)
    )
    mass = over_banks(jnp.add, mass)
    extra = jnp.where(present, mixed_exp * slope, 0.0)
    coef = queue_exp * INV_TEMP
    for h in range(SLOTS):
        coef = coef + jnp.where(index == pick[h:h + 1], extra[h:h + 1], 0.0)
    hi, lo = split(jnp.transpose(coef))
    blank = jnp.zeros((8, 128), f32)
    small = [key_exp * INV_TEMP, blank, jnp.where(own, 1.0, 0.0), blank, jnp.zeros((96, 128), f32)]
    small = jnp.transpose(jnp.concatenate(small, axis=0))
    lane = iota((OWN, 128), 1)
    product = functools.partial(jnp.dot, preferred_element_type=f32)
    sums = jnp.zeros((2 * OWN, PART), f32)
    few = jnp.zeros((OWN, 128), f32)
    keys = []
    for b in range(BANKS):
        at = slice(b * OWN, (b + 1) * OWN)
        bank_ref = (near_ref, far_ref)[b // 2]
        sums = sums + product(jnp.concatenate([hi[at], lo[at]], axis=0), bank_ref[b % 2, :ROWS])
        few = jnp.where(lane % KEYS // 2 == b, pltpu.roll(small[at], 2 * b, 1), few)
        keys.append(bank_ref[b % 2, ROWS:].astype(f32)[:2])
    keys = jnp.concatenate(keys + [jnp.zeros((KEYS - 8, PART), f32)], axis=0).astype(bf16)
    chosen = pltpu.roll(few, 128 - KEYS, 1)
    few_hi = few.astype(bf16).astype(f32)
    few = jnp.concatenate([few_hi, few - few_hi, chosen], axis=0).astype(bf16)[:, :KEYS]
    extras = product(few, keys)
    sums = (sums[:OWN] + sums[OWN:]) + (extras[:OWN] + extras[OWN:2 * OWN])
    out_ref[:, :PART], level = quantized(sums)
    out_ref[:, PART:2 * PART], key_level = quantized(extras[2 * OWN:])
    rows = jnp.concatenate([top, mass, positive, jnp.zeros((5, 128), f32)], axis=0)
    stats = spread(rows, jnp.where(iota((1, 128), 1) < 3, iota((1, 128), 1), -1))[:OWN]
    stats = jnp.where(lane == 3, level, jnp.where(lane == 4, key_level, jnp.where(lane == 5, over, stats)))
    pieces = jnp.floor(stats)
    rest = (stats - pieces) * FINE
    middle = jnp.floor(rest)
    last = jnp.floor((rest - middle) * FINE)
    middle = middle - 32768.0
    last = last - 32768.0
    block = jnp.where(lane < 8, pieces, jnp.where(lane < 16, pltpu.roll(middle, 8, 1), pltpu.roll(last, 16, 1)))
    out_ref[:, 2 * PART:] = jnp.where(lane < 24, block, 0.0).astype(jnp.int32).astype(jnp.int16)


def inner_kernel(parts_ref, query_ref, hidden_ref, gain_ref, out_ref, grad_ref):
    pieces = parts_ref[:, 2 * PART:].astype(jnp.int32).astype(f32)
    middle = pltpu.roll(pieces, 120, 1) + 32768.0
    last = pltpu.roll(pieces, 112, 1) + 32768.0
    stats = pieces + (middle + last / FINE) / FINE
    tops = stats[:, 0:1]
    positives = stats[:, 2:3]
    even = iota((OWN, 1), 0) % 2 == 0
    both = jnp.maximum(tops, positives)
    top = jnp.where(
        even,
        jnp.max(jnp.where(even, both, ABSENT), axis=0, keepdims=True),
        jnp.max(jnp.where(even, ABSENT, both), axis=0, keepdims=True),
    )
    scale = jnp.exp(tops - top)
    mass = stats[:, 1:2] * scale
    own = jnp.exp(positives - top)

    def folded(at, factor):
        rows = parts_ref[:, at:at + PART].astype(jnp.int32).astype(f32) * (factor / FULL)
        rows = (rows[:8] + rows[8:16]) + (rows[16:24] + rows[24:])
        return (rows[0:2] + rows[2:4]) + (rows[4:6] + rows[6:8])

    sums = folded(0, scale * jnp.exp(stats[:, 3:4]))
    key = folded(PART, jnp.exp(stats[:, 4:5]))
    others, full = [], []
    for mask in (even, jnp.logical_not(even)):
        others.append(jnp.sum(jnp.where(mask, mass, 0.0), axis=0, keepdims=True))
        full.append(others[-1] + jnp.sum(jnp.where(mask, own, 0.0), axis=0, keepdims=True))
    others = jnp.concatenate(others, axis=0)
    full = jnp.concatenate(full, axis=0)
    share = others / full
    sums = sums / full
    grad = LOSS_SCALE * (sums - key * (share * INV_TEMP))
    grad_ref[...] = grad
    query = query_ref[...]
    gain = gain_ref[...]
    along = jnp.sum(query * grad, axis=1, keepdims=True)
    rows = jnp.concatenate([grad * gain, query * gain, jnp.zeros((4, PART), f32)], axis=0)
    hi = rows.astype(bf16).astype(f32)
    mid = (rows - hi).astype(bf16).astype(f32)
    pieces = jnp.concatenate([hi, mid, rows - hi - mid, jnp.zeros((8, PART), f32)], axis=0).astype(bf16)
    dots = dot_t(pieces, hidden_ref[...])
    dots = dots[:8] + (dots[8:16] + dots[16:24])
    first = iota((1, 128), 1) < SEQ
    of_grad = jnp.where(first, dots[0:1], dots[1:2])
    of_query = jnp.where(first, dots[2:3], dots[3:4])
    of_along = jnp.where(first, along[0:1], along[1:2])
    row = iota((8, 128), 0)
    over = jnp.max(stats[:, 5:6], axis=0, keepdims=True)
    block = jnp.where(
        row == 0, of_grad, jnp.where(row == 1, of_query, jnp.where(row == 2, of_along, over))
    )
    for peer in range(8):
        out_ref[peer] = block


def output_kernel(
    sums_ref, grad_ref, query_ref, stat_ref, hidden_ref, gain_ref, out_far, over_far, out_ref, over_ref, sems
):
    total = sums_ref[0]
    for peer in range(1, 8):
        total = total + sums_ref[peer]
    inverse = stat_ref[0:1]
    length = stat_ref[1:2]
    along = total[2:3]
    over_ref[0] = (jnp.max(total[3:4]) > 0.5).astype(jnp.int32)
    mark = pltpu.make_async_copy(over_ref, over_far, sems.at[2])
    mark.start()
    inner = inverse * (total[0:1] - along * total[1:2]) / (length * WIDTH)
    inverse_column = column(inverse)
    slide = column(inverse * inverse * inner) / SEQ
    gain = gain_ref[...]
    copies = [mark]
    for q in range(2):
        at = q * SEQ
        scaled = (
            gain * (grad_ref[q:q + 1] - along[:, at:at + 1] * query_ref[q:q + 1])
            / (length[:, at:at + 1] * SEQ)
        )
        out_ref[at:at + SEQ] = (
            inverse_column[at:at + SEQ] * scaled
            - hidden_ref[at:at + SEQ].astype(f32) * slide[at:at + SEQ]
        )
        part = pl.ds(at, SEQ)
        copies.append(pltpu.make_async_copy(out_ref.at[part], out_far.at[part], sems.at[q]))
        copies[-1].start()
    for copy in copies:
        copy.wait()


def shape(dims, kind=f32):
    return jax.ShapeDtypeStruct(dims, kind)


def shards(hidden, gain, keys, queue, positive, mix_rows, mix_weight):
    tokens = hidden.reshape(TOKENS, PART)
    gain = gain.reshape(1, PART)
    squares, bank = call(
        squares_kernel, [shape((8, 40, 128)), shape((BANK, PART), bf16)], tokens, queue, gain, keys,
        far=range(4), vmem=63 << 20,
        scratch=[
            pltpu.VMEM((TOKENS, PART), bf16),
            pltpu.VMEM((1, PART), f32),
            pltpu.VMEM((2, PART), bf16),
            pltpu.SemaphoreType.DMA((4,)),
        ],
    )
    swap = [(0, 1), (1, 0)]
    squares = lax.all_to_all(squares, PIPE, 0, 0)
    own, squares = lax.optimization_barrier((bank, squares))
    came = lax.ppermute(own, "xh", swap)
    payload, query, stat = call(
        query_kernel, [shape((16, 16, 128), bf16), shape((2, PART)), shape((8, 128))], squares, tokens, gain
    )
    gathered = lax.all_to_all(payload, "z", 0, 0)
    near = call(pair_kernel, shape((2, BANK, PART), bf16), own, came, gathered)
    far = lax.ppermute(near, "c", swap)
    dots, queries, index = call(
        near_kernel, [shape((BANK, 128)), shape((OWN, PART), bf16), shape((40, 128))],
        gathered, near, mix_rows.T, mix_weight.T, positive.reshape(1, QUERIES),
        scratch=[pltpu.VMEM((OWN * CHUNKS, 128), f32)],
    )
    coded, exact = call(
        far_kernel, [shape((8, SENT, 128), jnp.int16), shape((BANK, 128))], dots, queries, far
    )
    coded = lax.all_to_all(coded, PIPE, 0, 0)
    parts = call(coded_grad_kernel, shape((OWN, EXT), jnp.int16), coded, index, near, far)

    def finish(parts):
        parts = lax.all_to_all(parts.reshape(16, 2, EXT), "z", 0, 0).reshape(OWN, EXT)
        sums, grad = call(
            inner_kernel, [shape((8, 8, 128)), shape((2, PART))], parts, query, tokens, gain
        )
        sums = lax.all_to_all(sums, PIPE, 0, 0)
        return call(
            output_kernel, [shape((TOKENS, PART)), shape((1,), jnp.int32)],
            sums, grad, query, stat, tokens, gain, far_outs=(0, 1),
            scratch=[
                pltpu.VMEM((TOKENS, PART), f32), pltpu.SMEM((1,), jnp.int32), pltpu.SemaphoreType.DMA((3,))
            ],
        )

    def repeat(state):
        dots = jnp.sum(lax.all_to_all(jnp.broadcast_to(state[2], (8, BANK, 128)), PIPE, 0, 0), axis=0)
        parts = call(exact_grad_kernel, shape((OWN, EXT), jnp.int16), dots, index, near, far)
        return (*finish(parts), dots)

    out = lax.while_loop(lambda state: state[1][0] > 0, repeat, (*finish(parts), exact))[0]
    return out.reshape(2, SEQ, PART)


def solution(mesh):
    fine = Mesh(mesh.devices.reshape(2, 16, 2, 4, 2), ("xh", "z", "c", "y", "xl"))
    dp = ("xh", "z", "c")
    placed = (P(dp, None, PIPE), P(PIPE), P(dp, PIPE), P(dp, PIPE), P(), P(), P())
    return jax.shard_map(
        shards, mesh=fine, in_specs=placed, out_specs=P(dp, None, PIPE), check_vma=False
    )
```

```python
import functools
import math

import jax
import jax.numpy as jnp
from jax import lax
from jax.experimental import pallas as pl
from jax.experimental.pallas import tpu as pltpu
from jax.sharding import Mesh, PartitionSpec as P

NORM_EPS = 1e-05
MIX_EPS = 1e-06
INV_TEMP = 20.0
LOSS_SCALE = 2048.0
WIDTH = 8192
PART = 1024
CHUNKS = 8
SEQ = 64
TOKENS = 128
QUERIES = 128
ROWS = 256
KEYS = 16
BANK = ROWS + KEYS
BANKS = 4
OWN = 32
SLOTS = 16
EXT = 2 * PART + 128
ABSENT = -30000.0
FINE = 65536.0
FULL = 32000.0
SENT = ROWS + 32
MOST = 0.5
PIPE = ("y", "xl")
VMEM = 24 << 20

f32 = jnp.float32
bf16 = jnp.bfloat16


def dot_t(a, b):
    return lax.dot_general(a, b, (((1,), (1,)), ((), ())), preferred_element_type=f32)


def split(a):
    hi = a.astype(bf16)
    return hi, (a - hi.astype(f32)).astype(bf16)


def iota(shape, dim):
    return lax.broadcasted_iota(jnp.int32, shape, dim)


def padded(keys):
    return jnp.concatenate([keys.astype(f32), jnp.zeros((KEYS - 2, PART), f32)], axis=0).astype(bf16)


def own_lanes(rows):
    old, new = iota((128, 128), 0), iota((128, 128), 1) % OWN
    place = ((lax.axis_index("xh") * 16 + new // 2) * 2 + lax.axis_index("c")) * 2 + new % 2
    chosen = jnp.where(old == place, 1.0, 0.0).astype(bf16)
    hi = rows.astype(bf16)
    rest = rows - hi.astype(f32)
    mid = rest.astype(bf16)
    low = (rest - mid.astype(f32)).astype(bf16)
    product = functools.partial(jnp.dot, preferred_element_type=f32)
    return product(hi, chosen) + (product(mid, chosen) + product(low, chosen))


def spread(rows, lanes):
    hi = rows.astype(bf16).astype(f32)
    mid = (rows - hi).astype(bf16).astype(f32)
    pieces = jnp.concatenate([hi, mid, rows - hi - mid, jnp.zeros((8, 128), f32)], axis=0).astype(bf16)
    chosen = jnp.where(iota((32, 128), 0) % 8 == lanes, 1.0, 0.0).astype(bf16)
    return lax.dot_general(pieces, chosen, (((0,), (0,)), ((), ())), preferred_element_type=f32)


def over_banks(op, row):
    block = jnp.broadcast_to(row, (8, 128))
    block = op(block, pltpu.roll(block, 64, 1))
    return op(block, pltpu.roll(block, 32, 1))[:1]


def whole(a):
    return jnp.floor(a + 0.5).astype(jnp.int32)


def diagonal(square):
    n = square.shape[0]
    on = iota((n, n), 0) == iota((n, n), 1)
    return jnp.sum(jnp.where(on, square, 0.0), axis=0, keepdims=True)


def flat(tall):
    on = iota((128, 128), 0) == iota((128, 128), 1)
    return jnp.sum(jnp.where(on, tall, 0.0), axis=0, keepdims=True)


def column(row):
    on = iota((128, 128), 0) == iota((128, 128), 1)
    return jnp.sum(jnp.where(on, row, 0.0), axis=1, keepdims=True)


def fold(row):
    return jnp.concatenate([row[:, c * 128:(c + 1) * 128] for c in range(CHUNKS)], axis=0)


def unfold(block):
    return jnp.concatenate([block[c:c + 1] for c in range(CHUNKS)], axis=1)


def call(kernel, outs, *args, far=(), far_outs=(), scratch=(), vmem=VMEM):
    def place(i, far):
        return pl.BlockSpec(memory_space=pltpu.HBM if i in far else pltpu.VMEM)

    many = isinstance(outs, (list, tuple))
    return pl.pallas_call(
        kernel,
        out_shape=outs,
        in_specs=[place(i, far) for i in range(len(args))],
        out_specs=[place(i, far_outs) for i in range(len(outs))] if many else place(0, far_outs),
        scratch_shapes=scratch,
        compiler_params=pltpu.CompilerParams(vmem_limit_bytes=vmem),
    )(*args)


def squares_kernel(
    hidden_far, queue_far, gain_far, keys_far, out_ref, bank_ref, hidden_ref, gain_ref, keys_ref, sems
):
    copies = [
        pltpu.make_async_copy(source, target, sems.at[i])
        for i, (source, target) in enumerate((
            (keys_far, keys_ref),
            (gain_far, gain_ref),
            (hidden_far, hidden_ref),
            (queue_far, bank_ref.at[pl.ds(0, ROWS)]),
        ))
    ]
    for copy in copies:
        copy.start()
    for copy in copies[:-1]:
        copy.wait()
    bank_ref[ROWS:] = padded(keys_ref[...])
    x = hidden_ref[...]
    weighted = x.astype(f32) * (gain_ref[...] * gain_ref[...])
    hi, lo = split(weighted)
    products = dot_t(jnp.concatenate([hi, lo, x], axis=0), x)
    gram = products[:128] + products[128:256]
    up = iota((SEQ, 128), 0) < iota((SEQ, 128), 1)
    both = jnp.where(up, gram[:SEQ], pltpu.roll(gram[SEQ:], SEQ, 1))
    left = iota((32, 128), 1) < SEQ
    packed = jnp.where(left, both[:32], pltpu.roll(both[32:], SEQ, 1))
    token = diagonal(products[256:])
    diag = diagonal(gram)
    row = iota((8, 128), 0)
    sums = jnp.where(row == 0, token, jnp.where(row == 1, diag, 0.0))
    for peer in range(8):
        out_ref[peer, :32] = packed
        out_ref[peer, 32:] = sums
    copies[-1].wait()


def query_kernel(sums_ref, hidden_ref, gain_ref, payload_ref, query_ref, stat_ref):
    total = sums_ref[0]
    for peer in range(1, 8):
        total = total + sums_ref[peer]
    token = total[32:33]
    diag = total[33:34]
    inverse = lax.rsqrt(token / WIDTH + NORM_EPS)
    inverse_column = column(inverse)
    first = iota((1, 128), 1) < SEQ
    both = jnp.concatenate([total[:32], pltpu.roll(total[:32], SEQ, 1)], axis=0)
    t, u = iota((SEQ, 128), 0), iota((SEQ, 128), 1)
    second = pltpu.roll(jnp.broadcast_to(inverse, (8, 128)), SEQ, 1)[:1]
    pair = jnp.where(t < u, inverse_column[:SEQ] * inverse, inverse_column[SEQ:] * second)
    pair = jnp.where((t != u) & (u < SEQ), pair * both, 0.0)
    own = diag * inverse * inverse
    lengths = []
    for mask, on in ((first, t < u), (jnp.logical_not(first), t > u)):
        off = jnp.sum(jnp.where(on, pair, 0.0), axis=0, keepdims=True)
        square = jnp.sum(2.0 * off + jnp.where(mask, own, 0.0), axis=1, keepdims=True)
        lengths.append(jnp.sqrt(square) / SEQ)
    weighted = hidden_ref[...].astype(f32) * inverse_column
    gain = gain_ref[...]
    blocks = []
    for q in range(2):
        pooled = jnp.sum(weighted[q * SEQ:(q + 1) * SEQ], axis=0, keepdims=True) * gain / SEQ
        query = pooled / lengths[q]
        query_ref[q:q + 1] = query
        blocks.append(fold(query))
    half = jnp.concatenate(blocks, axis=0).astype(bf16)
    for z in range(16):
        payload_ref[z] = half
    length_row = jnp.where(first, lengths[0], lengths[1])
    stat_ref[...] = jnp.where(iota((8, 128), 0) == 0, inverse, length_row)


def pair_kernel(own_ref, came_ref, after_ref, out_ref):
    del after_ref
    out_ref[0] = own_ref[...]
    out_ref[1] = came_ref[...]


def bank_dots(bank_ref, queries):
    dots, squares = [], []
    for b in range(2):
        dots.append(dot_t(bank_ref[b], queries))
        rows = bank_ref[b, :ROWS].astype(f32)
        part = rows[:, :128] * rows[:, :128]
        for c in range(1, CHUNKS):
            chunk = rows[:, c * 128:(c + 1) * 128]
            part = part + chunk * chunk
        total = jnp.sum(part, axis=1, keepdims=True)
        squares += [flat(total[:128]), flat(total[128:])]
    return dots, squares


def near_kernel(
    gathered_ref, near_ref, pick_ref, weight_ref, positive_ref, out_ref, queries_ref, index_ref, rows_ref
):
    indices = [
        pick_ref[...].astype(f32),
        weight_ref[...],
        jnp.broadcast_to(positive_ref[...].astype(f32), (8, 128)),
    ]
    index_ref[...] = own_lanes(jnp.concatenate(indices, axis=0))
    rows_ref[...] = gathered_ref[...].astype(f32).reshape(OWN * CHUNKS, 128)
    queries = jnp.concatenate(
        [rows_ref[pl.ds(c, OWN, stride=CHUNKS), :].astype(bf16) for c in range(CHUNKS)], axis=1
    )
    queries_ref[...] = queries
    dots, squares = bank_dots(near_ref, queries)
    out_ref[:ROWS + 8] = jnp.concatenate([d[:ROWS + 8] for d in dots] * 2, axis=1)
    out_ref[ROWS + 8:] = jnp.concatenate(squares * 2, axis=0)


def pieces_of(values):
    whole_part = jnp.floor(values)
    rest = (values - whole_part) * FINE
    middle = jnp.floor(rest)
    last = jnp.floor((rest - middle) * FINE)
    return whole_part, middle - 32768.0, last - 32768.0


def value_of(whole_part, middle, last):
    return whole_part + (middle + 32768.0 + (last + 32768.0) / FINE) / FINE


def far_kernel(part_ref, queries_ref, far_ref, out_ref, exact_ref):
    dots, squares = bank_dots(far_ref, queries_ref[...])
    dots = jnp.concatenate([d[:ROWS + 8] for d in dots] * 2, axis=1)
    dots = jnp.where(iota((ROWS + 8, 128), 1) < 2 * OWN, part_ref[:ROWS + 8], dots)
    squares = jnp.concatenate([part_ref[ROWS + 8:ROWS + 12]] + squares, axis=0)
    exact_ref[:ROWS + 8] = dots
    exact_ref[ROWS + 8:] = squares
    most = jnp.maximum(jnp.max(jnp.abs(dots), axis=0, keepdims=True), 1e-30)
    level = jnp.floor(jnp.log(most) * FINE + 0.5) / FINE
    coded = jnp.floor(dots * (FULL * jnp.exp(-level)) + 0.5)
    scale = list(pieces_of(level)[:2])
    tail = list(pieces_of(squares)) + [coded[ROWS:ROWS + 2]] + scale + [jnp.zeros((4, 128), f32)]
    tail = jnp.concatenate(tail, axis=0)
    coded = coded[:ROWS].astype(jnp.int32).astype(jnp.int16)
    tail = tail.astype(jnp.int32).astype(jnp.int16)
    for peer in range(8):
        out_ref[peer, :ROWS] = coded
        out_ref[peer, ROWS:] = tail


def levels_of(coded_ref):
    levels = []
    for peer in range(8):
        tail = coded_ref[peer, ROWS:].astype(jnp.int32).astype(f32)
        levels.append(tail[26:27] + (tail[27:28] + 32768.0) / FINE)
    return levels, jnp.max(functools.reduce(jnp.maximum, levels), axis=1, keepdims=True) > math.log(MOST)


def decoded(coded_ref):
    levels, over = levels_of(coded_ref)
    queue_dots = jnp.zeros((ROWS, 128), f32)
    rest = jnp.zeros((16, 128), f32)
    for peer in range(8):
        tail = coded_ref[peer, ROWS:].astype(jnp.int32).astype(f32)
        factor = jnp.exp(levels[peer]) / FULL
        queue_dots = queue_dots + coded_ref[peer, :ROWS].astype(jnp.int32).astype(f32) * factor
        squares = value_of(tail[:8], tail[8:16], tail[16:24])
        rest = rest + jnp.concatenate([tail[24:] * factor, squares], axis=0)
    return jnp.concatenate([queue_dots, rest], axis=0), over


def quantized(rows):
    most = jnp.maximum(jnp.max(jnp.abs(rows), axis=1, keepdims=True), 1e-30)
    level = jnp.floor(jnp.log(most) * FINE + 0.5) / FINE
    return whole(rows * (FULL * jnp.exp(-level))).astype(jnp.int16), level


def bank_of(shard):
    across = (shard // 32 != lax.axis_index("xh")).astype(jnp.int32)
    beside = (shard % 2 != lax.axis_index("c")).astype(jnp.int32)
    return jnp.where(shard // 2 % 16 == lax.axis_index("z"), across + 2 * beside, -1)


def coded_grad_kernel(coded_ref, index_ref, near_ref, far_ref, out_ref):
    dots, over = decoded(coded_ref)
    grad_parts(dots, jnp.where(over, 1.0, 0.0), index_ref, near_ref, far_ref, out_ref)


def exact_grad_kernel(dots_ref, index_ref, near_ref, far_ref, out_ref):
    grad_parts(dots_ref[...], jnp.zeros((1, 1), f32), index_ref, near_ref, far_ref, out_ref)


def grad_parts(dots, over, index_ref, near_ref, far_ref, out_ref):
    queue_dots = dots[:ROWS]
    key_dots = dots[ROWS:ROWS + 8]
    group = iota((1, 128), 1) // OWN
    square = jnp.concatenate([spread(dots[ROWS + 8:], 2 * group + half) for half in range(2)], axis=0)
    index = iota((ROWS, 128), 0)
    rows = whole(index_ref[:16])
    present = bank_of(rows // ROWS) == group
    pick = jnp.where(present, rows % ROWS, -8)
    beta = index_ref[16:32]
    target = whole(index_ref[32:33])
    held = bank_of(target // 2) == group
    target = jnp.where(held, target % 2, -1)
    tile, inside = pick // 8, pick % 8
    sublane = iota((8, 128), 0)
    cosines, squares = [], []
    for h in range(SLOTS):
        chosen = jnp.zeros((8, 128), f32)
        scale = jnp.zeros((8, 128), f32)
        for t in range(ROWS // 8):
            on = tile[h:h + 1] == t
            chosen = jnp.where(on, queue_dots[8 * t:8 * t + 8], chosen)
            scale = jnp.where(on, square[8 * t:8 * t + 8], scale)
        here = sublane == inside[h:h + 1]
        cosines.append(jnp.sum(jnp.where(here, chosen, 0.0), axis=0, keepdims=True))
        squares.append(jnp.sum(jnp.where(here, scale, 0.0), axis=0, keepdims=True))
    cosine = jnp.concatenate(cosines, axis=0)
    picked = jnp.concatenate(squares, axis=0)
    rest = 1.0 - beta
    numer = beta + rest * cosine
    radius_sq = beta * beta + rest * rest * picked + 2.0 * beta * rest * cosine + MIX_EPS
    radius_sq = jnp.where(present, radius_sq, 1.0)
    radius = jnp.sqrt(radius_sq)
    mixed = numer * INV_TEMP / radius
    slope = (rest - numer * beta * rest / radius_sq) * INV_TEMP / radius
    low = -1e30
    mixed = jnp.where(present, mixed, low)
    queue_scores = queue_dots * INV_TEMP
    key_row = iota((8, 128), 0)
    own = key_row == target
    positive = jnp.sum(jnp.where(own, key_dots * INV_TEMP, 0.0), axis=0, keepdims=True)
    positive = over_banks(jnp.maximum, jnp.where(held, positive, ABSENT))
    other = (key_row < 2) & jnp.logical_not(own)
    key_scores = jnp.where(other, key_dots * INV_TEMP, low)
    top = jnp.maximum(
        jnp.maximum(
            jnp.max(queue_scores, axis=0, keepdims=True), jnp.max(key_scores, axis=0, keepdims=True)
        ),
        jnp.max(mixed, axis=0, keepdims=True),
    )
    top = over_banks(jnp.maximum, top)
    queue_exp = jnp.exp(queue_scores - top)
    key_exp = jnp.where(other, jnp.exp(key_scores - top), 0.0)
    mixed_exp = jnp.where(present, jnp.exp(mixed - top), 0.0)
    mass = (
        jnp.sum(queue_exp, axis=0, keepdims=True)
        + jnp.sum(key_exp, axis=0, keepdims=True)
        + jnp.sum(mixed_exp, axis=0, keepdims=True)
    )
    mass = over_banks(jnp.add, mass)
    extra = jnp.where(present, mixed_exp * slope, 0.0)
    coef = queue_exp * INV_TEMP
    for h in range(SLOTS):
        coef = coef + jnp.where(index == pick[h:h + 1], extra[h:h + 1], 0.0)
    hi, lo = split(jnp.transpose(coef))
    blank = jnp.zeros((8, 128), f32)
    small = [key_exp * INV_TEMP, blank, jnp.where(own, 1.0, 0.0), blank, jnp.zeros((96, 128), f32)]
    small = jnp.transpose(jnp.concatenate(small, axis=0))
    lane = iota((OWN, 128), 1)
    product = functools.partial(jnp.dot, preferred_element_type=f32)
    sums = jnp.zeros((2 * OWN, PART), f32)
    few = jnp.zeros((OWN, 128), f32)
    keys = []
    for b in range(BANKS):
        at = slice(b * OWN, (b + 1) * OWN)
        bank_ref = (near_ref, far_ref)[b // 2]
        sums = sums + product(jnp.concatenate([hi[at], lo[at]], axis=0), bank_ref[b % 2, :ROWS])
        few = jnp.where(lane % KEYS // 2 == b, pltpu.roll(small[at], 2 * b, 1), few)
        keys.append(bank_ref[b % 2, ROWS:].astype(f32)[:2])
    keys = jnp.concatenate(keys + [jnp.zeros((KEYS - 8, PART), f32)], axis=0).astype(bf16)
    chosen = pltpu.roll(few, 128 - KEYS, 1)
    few_hi = few.astype(bf16).astype(f32)
    few = jnp.concatenate([few_hi, few - few_hi, chosen], axis=0).astype(bf16)[:, :KEYS]
    extras = product(few, keys)
    sums = (sums[:OWN] + sums[OWN:]) + (extras[:OWN] + extras[OWN:2 * OWN])
    out_ref[:, :PART], level = quantized(sums)
    out_ref[:, PART:2 * PART], key_level = quantized(extras[2 * OWN:])
    rows = jnp.concatenate([top, mass, positive, jnp.zeros((5, 128), f32)], axis=0)
    stats = spread(rows, jnp.where(iota((1, 128), 1) < 3, iota((1, 128), 1), -1))[:OWN]
    stats = jnp.where(lane == 3, level, jnp.where(lane == 4, key_level, jnp.where(lane == 5, over, stats)))
    pieces = jnp.floor(stats)
    rest = (stats - pieces) * FINE
    middle = jnp.floor(rest)
    last = jnp.floor((rest - middle) * FINE)
    middle = middle - 32768.0
    last = last - 32768.0
    block = jnp.where(lane < 8, pieces, jnp.where(lane < 16, pltpu.roll(middle, 8, 1), pltpu.roll(last, 16, 1)))
    out_ref[:, 2 * PART:] = jnp.where(lane < 24, block, 0.0).astype(jnp.int32).astype(jnp.int16)


def inner_kernel(parts_ref, query_ref, hidden_ref, gain_ref, out_ref, grad_ref):
    pieces = parts_ref[:, 2 * PART:].astype(jnp.int32).astype(f32)
    middle = pltpu.roll(pieces, 120, 1) + 32768.0
    last = pltpu.roll(pieces, 112, 1) + 32768.0
    stats = pieces + (middle + last / FINE) / FINE
    tops = stats[:, 0:1]
    positives = stats[:, 2:3]
    even = iota((OWN, 1), 0) % 2 == 0
    both = jnp.maximum(tops, positives)
    top = jnp.where(
        even,
        jnp.max(jnp.where(even, both, ABSENT), axis=0, keepdims=True),
        jnp.max(jnp.where(even, ABSENT, both), axis=0, keepdims=True),
    )
    scale = jnp.exp(tops - top)
    mass = stats[:, 1:2] * scale
    own = jnp.exp(positives - top)

    def folded(at, factor):
        rows = parts_ref[:, at:at + PART].astype(jnp.int32).astype(f32) * (factor / FULL)
        rows = (rows[:8] + rows[8:16]) + (rows[16:24] + rows[24:])
        return (rows[0:2] + rows[2:4]) + (rows[4:6] + rows[6:8])

    sums = folded(0, scale * jnp.exp(stats[:, 3:4]))
    key = folded(PART, jnp.exp(stats[:, 4:5]))
    others, full = [], []
    for mask in (even, jnp.logical_not(even)):
        others.append(jnp.sum(jnp.where(mask, mass, 0.0), axis=0, keepdims=True))
        full.append(others[-1] + jnp.sum(jnp.where(mask, own, 0.0), axis=0, keepdims=True))
    others = jnp.concatenate(others, axis=0)
    full = jnp.concatenate(full, axis=0)
    share = others / full
    sums = sums / full
    grad = LOSS_SCALE * (sums - key * (share * INV_TEMP))
    grad_ref[...] = grad
    query = query_ref[...]
    gain = gain_ref[...]
    along = jnp.sum(query * grad, axis=1, keepdims=True)
    rows = jnp.concatenate([grad * gain, query * gain, jnp.zeros((4, PART), f32)], axis=0)
    hi = rows.astype(bf16).astype(f32)
    mid = (rows - hi).astype(bf16).astype(f32)
    pieces = jnp.concatenate([hi, mid, rows - hi - mid, jnp.zeros((8, PART), f32)], axis=0).astype(bf16)
    dots = dot_t(pieces, hidden_ref[...])
    dots = dots[:8] + (dots[8:16] + dots[16:24])
    first = iota((1, 128), 1) < SEQ
    of_grad = jnp.where(first, dots[0:1], dots[1:2])
    of_query = jnp.where(first, dots[2:3], dots[3:4])
    of_along = jnp.where(first, along[0:1], along[1:2])
    row = iota((8, 128), 0)
    over = jnp.max(stats[:, 5:6], axis=0, keepdims=True)
    block = jnp.where(
        row == 0, of_grad, jnp.where(row == 1, of_query, jnp.where(row == 2, of_along, over))
    )
    for peer in range(8):
        out_ref[peer] = block


def output_kernel(
    sums_ref, grad_ref, query_ref, stat_ref, hidden_ref, gain_ref, out_far, over_far, out_ref, over_ref, sems
):
    total = sums_ref[0]
    for peer in range(1, 8):
        total = total + sums_ref[peer]
    inverse = stat_ref[0:1]
    length = stat_ref[1:2]
    along = total[2:3]
    over_ref[0] = (jnp.max(total[3:4]) > 0.5).astype(jnp.int32)
    mark = pltpu.make_async_copy(over_ref, over_far, sems.at[2])
    mark.start()
    inner = inverse * (total[0:1] - along * total[1:2]) / (length * WIDTH)
    inverse_column = column(inverse)
    slide = column(inverse * inverse * inner) / SEQ
    gain = gain_ref[...]
    copies = [mark]
    for q in range(2):
        at = q * SEQ
        scaled = (
            gain * (grad_ref[q:q + 1] - along[:, at:at + 1] * query_ref[q:q + 1])
            / (length[:, at:at + 1] * SEQ)
        )
        out_ref[at:at + SEQ] = (
            inverse_column[at:at + SEQ] * scaled
            - hidden_ref[at:at + SEQ].astype(f32) * slide[at:at + SEQ]
        )
        part = pl.ds(at, SEQ)
        copies.append(pltpu.make_async_copy(out_ref.at[part], out_far.at[part], sems.at[q]))
        copies[-1].start()
    for copy in copies:
        copy.wait()


def shape(dims, kind=f32):
    return jax.ShapeDtypeStruct(dims, kind)


def shards(hidden, gain, keys, queue, positive, mix_rows, mix_weight):
    tokens = hidden.reshape(TOKENS, PART)
    gain = gain.reshape(1, PART)
    squares, bank = call(
        squares_kernel, [shape((8, 40, 128)), shape((BANK, PART), bf16)], tokens, queue, gain, keys,
        far=range(4), vmem=63 << 20,
        scratch=[
            pltpu.VMEM((TOKENS, PART), bf16),
            pltpu.VMEM((1, PART), f32),
            pltpu.VMEM((2, PART), bf16),
            pltpu.SemaphoreType.DMA((4,)),
        ],
    )
    swap = [(0, 1), (1, 0)]
    squares = lax.all_to_all(squares, PIPE, 0, 0)
    own, squares = lax.optimization_barrier((bank, squares))
    came = lax.ppermute(own, "xh", swap)
    payload, query, stat = call(
        query_kernel, [shape((16, 16, 128), bf16), shape((2, PART)), shape((8, 128))], squares, tokens, gain
    )
    gathered = lax.all_to_all(payload, "z", 0, 0)
    near = call(pair_kernel, shape((2, BANK, PART), bf16), own, came, gathered)
    far = lax.ppermute(near, "c", swap)
    dots, queries, index = call(
        near_kernel, [shape((BANK, 128)), shape((OWN, PART), bf16), shape((40, 128))],
        gathered, near, mix_rows.T, mix_weight.T, positive.reshape(1, QUERIES),
        scratch=[pltpu.VMEM((OWN * CHUNKS, 128), f32)],
    )
    coded, exact = call(
        far_kernel, [shape((8, SENT, 128), jnp.int16), shape((BANK, 128))], dots, queries, far
    )
    coded = lax.all_to_all(coded, PIPE, 0, 0)
    parts = call(coded_grad_kernel, shape((OWN, EXT), jnp.int16), coded, index, near, far)

    def finish(parts):
        parts = lax.all_to_all(parts.reshape(16, 2, EXT), "z", 0, 0).reshape(OWN, EXT)
        sums, grad = call(
            inner_kernel, [shape((8, 8, 128)), shape((2, PART))], parts, query, tokens, gain
        )
        sums = lax.all_to_all(sums, PIPE, 0, 0)
        return call(
            output_kernel, [shape((TOKENS, PART)), shape((1,), jnp.int32)],
            sums, grad, query, stat, tokens, gain, far_outs=(0, 1),
            scratch=[
                pltpu.VMEM((TOKENS, PART), f32), pltpu.SMEM((1,), jnp.int32), pltpu.SemaphoreType.DMA((3,))
            ],
        )

    def repeat(state):
        dots = jnp.sum(lax.all_to_all(jnp.broadcast_to(state[2], (8, BANK, 128)), PIPE, 0, 0), axis=0)
        parts = call(exact_grad_kernel, shape((OWN, EXT), jnp.int16), dots, index, near, far)
        return (*finish(parts), dots)

    out = lax.while_loop(lambda state: state[1][0] > 0, repeat, (*finish(parts), exact))[0]
    return out.reshape(2, SEQ, PART)


def solution(mesh):
    fine = Mesh(mesh.devices.reshape(2, 16, 2, 4, 2), ("xh", "z", "c", "y", "xl"))
    dp = ("xh", "z", "c")
    placed = (P(dp, None, PIPE), P(PIPE), P(dp, PIPE), P(dp, PIPE), P(), P(), P())
    return jax.shard_map(
        shards, mesh=fine, in_specs=placed, out_specs=P(dp, None, PIPE), check_vma=False
    )
```

```python
import functools
import math

import jax
import jax.numpy as jnp
from jax import lax
from jax.experimental import pallas as pl
from jax.experimental.pallas import tpu as pltpu
from jax.sharding import Mesh, PartitionSpec as P

NORM_EPS = 1e-05
MIX_EPS = 1e-06
INV_TEMP = 20.0
LOSS_SCALE = 2048.0
WIDTH = 8192
PART = 1024
CHUNKS = 8
SEQ = 64
TOKENS = 128
QUERIES = 128
ROWS = 256
KEYS = 16
BANK = ROWS + KEYS
BANKS = 4
OWN = 32
SLOTS = 16
EXT = 2 * PART + 128
ABSENT = -30000.0
FINE = 65536.0
FULL = 32000.0
SENT = ROWS + 32
MOST = 0.5
PIPE = ("y", "xl")
VMEM = 24 << 20

f32 = jnp.float32
bf16 = jnp.bfloat16


def dot_t(a, b):
    return lax.dot_general(a, b, (((1,), (1,)), ((), ())), preferred_element_type=f32)


def split(a):
    hi = a.astype(bf16)
    return hi, (a - hi.astype(f32)).astype(bf16)


def iota(shape, dim):
    return lax.broadcasted_iota(jnp.int32, shape, dim)


def padded(keys):
    return jnp.concatenate([keys.astype(f32), jnp.zeros((KEYS - 2, PART), f32)], axis=0).astype(bf16)


def own_lanes(rows):
    old, new = iota((128, 128), 0), iota((128, 128), 1) % OWN
    place = ((lax.axis_index("xh") * 16 + new // 2) * 2 + lax.axis_index("c")) * 2 + new % 2
    chosen = jnp.where(old == place, 1.0, 0.0).astype(bf16)
    hi = rows.astype(bf16)
    rest = rows - hi.astype(f32)
    mid = rest.astype(bf16)
    low = (rest - mid.astype(f32)).astype(bf16)
    product = functools.partial(jnp.dot, preferred_element_type=f32)
    return product(hi, chosen) + (product(mid, chosen) + product(low, chosen))


def spread(rows, lanes):
    hi = rows.astype(bf16).astype(f32)
    mid = (rows - hi).astype(bf16).astype(f32)
    pieces = jnp.concatenate([hi, mid, rows - hi - mid, jnp.zeros((8, 128), f32)], axis=0).astype(bf16)
    chosen = jnp.where(iota((32, 128), 0) % 8 == lanes, 1.0, 0.0).astype(bf16)
    return lax.dot_general(pieces, chosen, (((0,), (0,)), ((), ())), preferred_element_type=f32)


def over_banks(op, row):
    block = jnp.broadcast_to(row, (8, 128))
    block = op(block, pltpu.roll(block, 64, 1))
    return op(block, pltpu.roll(block, 32, 1))[:1]


def whole(a):
    return jnp.floor(a + 0.5).astype(jnp.int32)


def diagonal(square):
    n = square.shape[0]
    on = iota((n, n), 0) == iota((n, n), 1)
    return jnp.sum(jnp.where(on, square, 0.0), axis=0, keepdims=True)


def flat(tall):
    on = iota((128, 128), 0) == iota((128, 128), 1)
    return jnp.sum(jnp.where(on, tall, 0.0), axis=0, keepdims=True)


def column(row):
    on = iota((128, 128), 0) == iota((128, 128), 1)
    return jnp.sum(jnp.where(on, row, 0.0), axis=1, keepdims=True)


def fold(row):
    return jnp.concatenate([row[:, c * 128:(c + 1) * 128] for c in range(CHUNKS)], axis=0)


def unfold(block):
    return jnp.concatenate([block[c:c + 1] for c in range(CHUNKS)], axis=1)


def call(kernel, outs, *args, far=(), far_outs=(), scratch=(), vmem=VMEM):
    def place(i, far):
        return pl.BlockSpec(memory_space=pltpu.HBM if i in far else pltpu.VMEM)

    many = isinstance(outs, (list, tuple))
    return pl.pallas_call(
        kernel,
        out_shape=outs,
        in_specs=[place(i, far) for i in range(len(args))],
        out_specs=[place(i, far_outs) for i in range(len(outs))] if many else place(0, far_outs),
        scratch_shapes=scratch,
        compiler_params=pltpu.CompilerParams(vmem_limit_bytes=vmem),
    )(*args)


def squares_kernel(
    hidden_far, queue_far, gain_far, keys_far, out_ref, bank_ref, hidden_ref, gain_ref, keys_ref, sems
):
    copies = [
        pltpu.make_async_copy(source, target, sems.at[i])
        for i, (source, target) in enumerate((
            (hidden_far, hidden_ref),
            (gain_far, gain_ref),
            (keys_far, keys_ref),
            (queue_far, bank_ref.at[pl.ds(0, ROWS)]),
        ))
    ]
    for copy in copies:
        copy.start()
    copies[0].wait()
    copies[1].wait()
    x = hidden_ref[...]
    weighted = x.astype(f32) * (gain_ref[...] * gain_ref[...])
    hi, lo = split(weighted)
    products = dot_t(jnp.concatenate([hi, lo, x], axis=0), x)
    gram = products[:128] + products[128:256]
    up = iota((SEQ, 128), 0) < iota((SEQ, 128), 1)
    both = jnp.where(up, gram[:SEQ], pltpu.roll(gram[SEQ:], SEQ, 1))
    left = iota((32, 128), 1) < SEQ
    packed = jnp.where(left, both[:32], pltpu.roll(both[32:], SEQ, 1))
    token = diagonal(products[256:])
    diag = diagonal(gram)
    row = iota((8, 128), 0)
    sums = jnp.where(row == 0, token, jnp.where(row == 1, diag, 0.0))
    for peer in range(8):
        out_ref[peer, :32] = packed
        out_ref[peer, 32:] = sums
    copies[2].wait()
    bank_ref[ROWS:] = padded(keys_ref[...])
    copies[3].wait()


def query_kernel(sums_ref, hidden_ref, gain_ref, payload_ref, query_ref, stat_ref):
    total = sums_ref[0]
    for peer in range(1, 8):
        total = total + sums_ref[peer]
    token = total[32:33]
    diag = total[33:34]
    inverse = lax.rsqrt(token / WIDTH + NORM_EPS)
    inverse_column = column(inverse)
    first = iota((1, 128), 1) < SEQ
    both = jnp.concatenate([total[:32], pltpu.roll(total[:32], SEQ, 1)], axis=0)
    t, u = iota((SEQ, 128), 0), iota((SEQ, 128), 1)
    second = pltpu.roll(jnp.broadcast_to(inverse, (8, 128)), SEQ, 1)[:1]
    pair = jnp.where(t < u, inverse_column[:SEQ] * inverse, inverse_column[SEQ:] * second)
    pair = jnp.where((t != u) & (u < SEQ), pair * both, 0.0)
    own = diag * inverse * inverse
    lengths = []
    for mask, on in ((first, t < u), (jnp.logical_not(first), t > u)):
        off = jnp.sum(jnp.where(on, pair, 0.0), axis=0, keepdims=True)
        square = jnp.sum(2.0 * off + jnp.where(mask, own, 0.0), axis=1, keepdims=True)
        lengths.append(jnp.sqrt(square) / SEQ)
    weighted = hidden_ref[...].astype(f32) * inverse_column
    gain = gain_ref[...]
    blocks = []
    for q in range(2):
        pooled = jnp.sum(weighted[q * SEQ:(q + 1) * SEQ], axis=0, keepdims=True) * gain / SEQ
        query = pooled / lengths[q]
        query_ref[q:q + 1] = query
        blocks.append(fold(query))
    half = jnp.concatenate(blocks, axis=0).astype(bf16)
    for z in range(16):
        payload_ref[z] = half
    length_row = jnp.where(first, lengths[0], lengths[1])
    stat_ref[...] = jnp.where(iota((8, 128), 0) == 0, inverse, length_row)


def pair_kernel(own_ref, came_ref, after_ref, out_ref):
    del after_ref
    out_ref[0] = own_ref[...]
    out_ref[1] = came_ref[...]


def bank_dots(bank_ref, queries):
    dots, squares = [], []
    for b in range(2):
        dots.append(dot_t(bank_ref[b], queries))
        rows = bank_ref[b, :ROWS].astype(f32)
        part = rows[:, :128] * rows[:, :128]
        for c in range(1, CHUNKS):
            chunk = rows[:, c * 128:(c + 1) * 128]
            part = part + chunk * chunk
        total = jnp.sum(part, axis=1, keepdims=True)
        squares += [flat(total[:128]), flat(total[128:])]
    return dots, squares


def near_kernel(
    gathered_ref, near_ref, pick_ref, weight_ref, positive_ref, out_ref, queries_ref, index_ref, rows_ref
):
    indices = [
        pick_ref[...].astype(f32),
        weight_ref[...],
        jnp.broadcast_to(positive_ref[...].astype(f32), (8, 128)),
    ]
    index_ref[...] = own_lanes(jnp.concatenate(indices, axis=0))
    rows_ref[...] = gathered_ref[...].astype(f32).reshape(OWN * CHUNKS, 128)
    queries = jnp.concatenate(
        [rows_ref[pl.ds(c, OWN, stride=CHUNKS), :].astype(bf16) for c in range(CHUNKS)], axis=1
    )
    queries_ref[...] = queries
    dots, squares = bank_dots(near_ref, queries)
    out_ref[:ROWS + 8] = jnp.concatenate([d[:ROWS + 8] for d in dots] * 2, axis=1)
    out_ref[ROWS + 8:] = jnp.concatenate(squares * 2, axis=0)


def pieces_of(values):
    whole_part = jnp.floor(values)
    rest = (values - whole_part) * FINE
    middle = jnp.floor(rest)
    last = jnp.floor((rest - middle) * FINE)
    return whole_part, middle - 32768.0, last - 32768.0


def value_of(whole_part, middle, last):
    return whole_part + (middle + 32768.0 + (last + 32768.0) / FINE) / FINE


def far_kernel(part_ref, queries_ref, far_ref, out_ref, exact_ref):
    dots, squares = bank_dots(far_ref, queries_ref[...])
    dots = jnp.concatenate([d[:ROWS + 8] for d in dots] * 2, axis=1)
    dots = jnp.where(iota((ROWS + 8, 128), 1) < 2 * OWN, part_ref[:ROWS + 8], dots)
    squares = jnp.concatenate([part_ref[ROWS + 8:ROWS + 12]] + squares, axis=0)
    exact_ref[:ROWS + 8] = dots
    exact_ref[ROWS + 8:] = squares
    most = jnp.maximum(jnp.max(jnp.abs(dots), axis=0, keepdims=True), 1e-30)
    level = jnp.floor(jnp.log(most) * FINE + 0.5) / FINE
    coded = jnp.floor(dots * (FULL * jnp.exp(-level)) + 0.5)
    scale = list(pieces_of(level)[:2])
    tail = list(pieces_of(squares)) + [coded[ROWS:ROWS + 2]] + scale + [jnp.zeros((4, 128), f32)]
    tail = jnp.concatenate(tail, axis=0)
    coded = coded[:ROWS].astype(jnp.int32).astype(jnp.int16)
    tail = tail.astype(jnp.int32).astype(jnp.int16)
    for peer in range(8):
        out_ref[peer, :ROWS] = coded
        out_ref[peer, ROWS:] = tail


def levels_of(coded_ref):
    levels = []
    for peer in range(8):
        tail = coded_ref[peer, ROWS:].astype(jnp.int32).astype(f32)
        levels.append(tail[26:27] + (tail[27:28] + 32768.0) / FINE)
    return levels, jnp.max(functools.reduce(jnp.maximum, levels), axis=1, keepdims=True) > math.log(MOST)


def decoded(coded_ref):
    levels, over = levels_of(coded_ref)
    queue_dots = jnp.zeros((ROWS, 128), f32)
    rest = jnp.zeros((16, 128), f32)
    for peer in range(8):
        tail = coded_ref[peer, ROWS:].astype(jnp.int32).astype(f32)
        factor = jnp.exp(levels[peer]) / FULL
        queue_dots = queue_dots + coded_ref[peer, :ROWS].astype(jnp.int32).astype(f32) * factor
        squares = value_of(tail[:8], tail[8:16], tail[16:24])
        rest = rest + jnp.concatenate([tail[24:] * factor, squares], axis=0)
    return jnp.concatenate([queue_dots, rest], axis=0), over


def quantized(rows):
    most = jnp.maximum(jnp.max(jnp.abs(rows), axis=1, keepdims=True), 1e-30)
    level = jnp.floor(jnp.log(most) * FINE + 0.5) / FINE
    return whole(rows * (FULL * jnp.exp(-level))).astype(jnp.int16), level


def bank_of(shard):
    across = (shard // 32 != lax.axis_index("xh")).astype(jnp.int32)
    beside = (shard % 2 != lax.axis_index("c")).astype(jnp.int32)
    return jnp.where(shard // 2 % 16 == lax.axis_index("z"), across + 2 * beside, -1)


def coded_grad_kernel(coded_ref, index_ref, near_ref, far_ref, out_ref):
    dots, over = decoded(coded_ref)
    grad_parts(dots, jnp.where(over, 1.0, 0.0), index_ref, near_ref, far_ref, out_ref)


def exact_grad_kernel(dots_ref, index_ref, near_ref, far_ref, out_ref):
    grad_parts(dots_ref[...], jnp.zeros((1, 1), f32), index_ref, near_ref, far_ref, out_ref)


def grad_parts(dots, over, index_ref, near_ref, far_ref, out_ref):
    queue_dots = dots[:ROWS]
    key_dots = dots[ROWS:ROWS + 8]
    group = iota((1, 128), 1) // OWN
    square = jnp.concatenate([spread(dots[ROWS + 8:], 2 * group + half) for half in range(2)], axis=0)
    index = iota((ROWS, 128), 0)
    rows = whole(index_ref[:16])
    present = bank_of(rows // ROWS) == group
    pick = jnp.where(present, rows % ROWS, -8)
    beta = index_ref[16:32]
    target = whole(index_ref[32:33])
    held = bank_of(target // 2) == group
    target = jnp.where(held, target % 2, -1)
    tile, inside = pick // 8, pick % 8
    sublane = iota((8, 128), 0)
    cosines, squares = [], []
    for h in range(SLOTS):
        chosen = jnp.zeros((8, 128), f32)
        scale = jnp.zeros((8, 128), f32)
        for t in range(ROWS // 8):
            on = tile[h:h + 1] == t
            chosen = jnp.where(on, queue_dots[8 * t:8 * t + 8], chosen)
            scale = jnp.where(on, square[8 * t:8 * t + 8], scale)
        here = sublane == inside[h:h + 1]
        cosines.append(jnp.sum(jnp.where(here, chosen, 0.0), axis=0, keepdims=True))
        squares.append(jnp.sum(jnp.where(here, scale, 0.0), axis=0, keepdims=True))
    cosine = jnp.concatenate(cosines, axis=0)
    picked = jnp.concatenate(squares, axis=0)
    rest = 1.0 - beta
    numer = beta + rest * cosine
    radius_sq = beta * beta + rest * rest * picked + 2.0 * beta * rest * cosine + MIX_EPS
    radius_sq = jnp.where(present, radius_sq, 1.0)
    radius = jnp.sqrt(radius_sq)
    mixed = numer * INV_TEMP / radius
    slope = (rest - numer * beta * rest / radius_sq) * INV_TEMP / radius
    low = -1e30
    mixed = jnp.where(present, mixed, low)
    queue_scores = queue_dots * INV_TEMP
    key_row = iota((8, 128), 0)
    own = key_row == target
    positive = jnp.sum(jnp.where(own, key_dots * INV_TEMP, 0.0), axis=0, keepdims=True)
    positive = over_banks(jnp.maximum, jnp.where(held, positive, ABSENT))
    other = (key_row < 2) & jnp.logical_not(own)
    key_scores = jnp.where(other, key_dots * INV_TEMP, low)
    top = jnp.maximum(
        jnp.maximum(
            jnp.max(queue_scores, axis=0, keepdims=True), jnp.max(key_scores, axis=0, keepdims=True)
        ),
        jnp.max(mixed, axis=0, keepdims=True),
    )
    top = over_banks(jnp.maximum, top)
    queue_exp = jnp.exp(queue_scores - top)
    key_exp = jnp.where(other, jnp.exp(key_scores - top), 0.0)
    mixed_exp = jnp.where(present, jnp.exp(mixed - top), 0.0)
    mass = (
        jnp.sum(queue_exp, axis=0, keepdims=True)
        + jnp.sum(key_exp, axis=0, keepdims=True)
        + jnp.sum(mixed_exp, axis=0, keepdims=True)
    )
    mass = over_banks(jnp.add, mass)
    extra = jnp.where(present, mixed_exp * slope, 0.0)
    coef = queue_exp * INV_TEMP
    for h in range(SLOTS):
        coef = coef + jnp.where(index == pick[h:h + 1], extra[h:h + 1], 0.0)
    hi, lo = split(jnp.transpose(coef))
    blank = jnp.zeros((8, 128), f32)
    small = [key_exp * INV_TEMP, blank, jnp.where(own, 1.0, 0.0), blank, jnp.zeros((96, 128), f32)]
    small = jnp.transpose(jnp.concatenate(small, axis=0))
    lane = iota((OWN, 128), 1)
    product = functools.partial(jnp.dot, preferred_element_type=f32)
    sums = jnp.zeros((2 * OWN, PART), f32)
    few = jnp.zeros((OWN, 128), f32)
    keys = []
    for b in range(BANKS):
        at = slice(b * OWN, (b + 1) * OWN)
        bank_ref = (near_ref, far_ref)[b // 2]
        sums = sums + product(jnp.concatenate([hi[at], lo[at]], axis=0), bank_ref[b % 2, :ROWS])
        few = jnp.where(lane % KEYS // 2 == b, pltpu.roll(small[at], 2 * b, 1), few)
        keys.append(bank_ref[b % 2, ROWS:].astype(f32)[:2])
    keys = jnp.concatenate(keys + [jnp.zeros((KEYS - 8, PART), f32)], axis=0).astype(bf16)
    chosen = pltpu.roll(few, 128 - KEYS, 1)
    few_hi = few.astype(bf16).astype(f32)
    few = jnp.concatenate([few_hi, few - few_hi, chosen], axis=0).astype(bf16)[:, :KEYS]
    extras = product(few, keys)
    sums = (sums[:OWN] + sums[OWN:]) + (extras[:OWN] + extras[OWN:2 * OWN])
    out_ref[:, :PART], level = quantized(sums)
    out_ref[:, PART:2 * PART], key_level = quantized(extras[2 * OWN:])
    rows = jnp.concatenate([top, mass, positive, jnp.zeros((5, 128), f32)], axis=0)
    stats = spread(rows, jnp.where(iota((1, 128), 1) < 3, iota((1, 128), 1), -1))[:OWN]
    stats = jnp.where(lane == 3, level, jnp.where(lane == 4, key_level, jnp.where(lane == 5, over, stats)))
    pieces = jnp.floor(stats)
    rest = (stats - pieces) * FINE
    middle = jnp.floor(rest)
    last = jnp.floor((rest - middle) * FINE)
    middle = middle - 32768.0
    last = last - 32768.0
    block = jnp.where(lane < 8, pieces, jnp.where(lane < 16, pltpu.roll(middle, 8, 1), pltpu.roll(last, 16, 1)))
    out_ref[:, 2 * PART:] = jnp.where(lane < 24, block, 0.0).astype(jnp.int32).astype(jnp.int16)


def inner_kernel(parts_ref, query_ref, hidden_ref, gain_ref, out_ref, grad_ref):
    pieces = parts_ref[:, 2 * PART:].astype(jnp.int32).astype(f32)
    middle = pltpu.roll(pieces, 120, 1) + 32768.0
    last = pltpu.roll(pieces, 112, 1) + 32768.0
    stats = pieces + (middle + last / FINE) / FINE
    tops = stats[:, 0:1]
    positives = stats[:, 2:3]
    even = iota((OWN, 1), 0) % 2 == 0
    both = jnp.maximum(tops, positives)
    top = jnp.where(
        even,
        jnp.max(jnp.where(even, both, ABSENT), axis=0, keepdims=True),
        jnp.max(jnp.where(even, ABSENT, both), axis=0, keepdims=True),
    )
    scale = jnp.exp(tops - top)
    mass = stats[:, 1:2] * scale
    own = jnp.exp(positives - top)

    def folded(at, factor):
        rows = parts_ref[:, at:at + PART].astype(jnp.int32).astype(f32) * (factor / FULL)
        rows = (rows[:8] + rows[8:16]) + (rows[16:24] + rows[24:])
        return (rows[0:2] + rows[2:4]) + (rows[4:6] + rows[6:8])

    sums = folded(0, scale * jnp.exp(stats[:, 3:4]))
    key = folded(PART, jnp.exp(stats[:, 4:5]))
    others, full = [], []
    for mask in (even, jnp.logical_not(even)):
        others.append(jnp.sum(jnp.where(mask, mass, 0.0), axis=0, keepdims=True))
        full.append(others[-1] + jnp.sum(jnp.where(mask, own, 0.0), axis=0, keepdims=True))
    others = jnp.concatenate(others, axis=0)
    full = jnp.concatenate(full, axis=0)
    share = others / full
    sums = sums / full
    grad = LOSS_SCALE * (sums - key * (share * INV_TEMP))
    grad_ref[...] = grad
    query = query_ref[...]
    gain = gain_ref[...]
    along = jnp.sum(query * grad, axis=1, keepdims=True)
    rows = jnp.concatenate([grad * gain, query * gain, jnp.zeros((4, PART), f32)], axis=0)
    hi = rows.astype(bf16).astype(f32)
    mid = (rows - hi).astype(bf16).astype(f32)
    pieces = jnp.concatenate([hi, mid, rows - hi - mid, jnp.zeros((8, PART), f32)], axis=0).astype(bf16)
    dots = dot_t(pieces, hidden_ref[...])
    dots = dots[:8] + (dots[8:16] + dots[16:24])
    first = iota((1, 128), 1) < SEQ
    of_grad = jnp.where(first, dots[0:1], dots[1:2])
    of_query = jnp.where(first, dots[2:3], dots[3:4])
    of_along = jnp.where(first, along[0:1], along[1:2])
    row = iota((8, 128), 0)
    over = jnp.max(stats[:, 5:6], axis=0, keepdims=True)
    block = jnp.where(
        row == 0, of_grad, jnp.where(row == 1, of_query, jnp.where(row == 2, of_along, over))
    )
    for peer in range(8):
        out_ref[peer] = block


def output_kernel(
    sums_ref, grad_ref, query_ref, stat_ref, hidden_ref, gain_ref, out_far, over_far, out_ref, over_ref, sems
):
    total = sums_ref[0]
    for peer in range(1, 8):
        total = total + sums_ref[peer]
    inverse = stat_ref[0:1]
    length = stat_ref[1:2]
    along = total[2:3]
    over_ref[0] = (jnp.max(total[3:4]) > 0.5).astype(jnp.int32)
    mark = pltpu.make_async_copy(over_ref, over_far, sems.at[0])
    mark.start()
    inner = inverse * (total[0:1] - along * total[1:2]) / (length * WIDTH)
    inverse_column = column(inverse)
    slide = column(inverse * inverse * inner) / SEQ
    gain = gain_ref[...]
    copies = [mark]
    for q in range(2):
        at = q * SEQ
        scaled = (
            gain * (grad_ref[q:q + 1] - along[:, at:at + 1] * query_ref[q:q + 1])
            / (length[:, at:at + 1] * SEQ)
        )
        for half in range(2):
            part = slice(at + half * 32, at + half * 32 + 32)
            out_ref[part] = inverse_column[part] * scaled - hidden_ref[part].astype(f32) * slide[part]
            rows = pl.ds(at + half * 32, 32)
            copies.append(pltpu.make_async_copy(out_ref.at[rows], out_far.at[rows], sems.at[1 + 2 * q + half]))
            copies[-1].start()
    for copy in copies:
        copy.wait()


def shape(dims, kind=f32):
    return jax.ShapeDtypeStruct(dims, kind)


def shards(hidden, gain, keys, queue, positive, mix_rows, mix_weight):
    tokens = hidden.reshape(TOKENS, PART)
    gain = gain.reshape(1, PART)
    squares, bank = call(
        squares_kernel, [shape((8, 40, 128)), shape((BANK, PART), bf16)], tokens, queue, gain, keys,
        far=range(4), vmem=63 << 20,
        scratch=[
            pltpu.VMEM((TOKENS, PART), bf16),
            pltpu.VMEM((1, PART), f32),
            pltpu.VMEM((2, PART), bf16),
            pltpu.SemaphoreType.DMA((4,)),
        ],
    )
    swap = [(0, 1), (1, 0)]
    squares = lax.all_to_all(squares, PIPE, 0, 0)
    own, squares = lax.optimization_barrier((bank, squares))
    came = lax.ppermute(own, "xh", swap)
    payload, query, stat = call(
        query_kernel, [shape((16, 16, 128), bf16), shape((2, PART)), shape((8, 128))], squares, tokens, gain
    )
    gathered = lax.all_to_all(payload, "z", 0, 0)
    near = call(pair_kernel, shape((2, BANK, PART), bf16), own, came, gathered)
    far = lax.ppermute(near, "c", swap)
    dots, queries, index = call(
        near_kernel, [shape((BANK, 128)), shape((OWN, PART), bf16), shape((40, 128))],
        gathered, near, mix_rows.T, mix_weight.T, positive.reshape(1, QUERIES),
        scratch=[pltpu.VMEM((OWN * CHUNKS, 128), f32)],
    )
    coded, exact = call(
        far_kernel, [shape((8, SENT, 128), jnp.int16), shape((BANK, 128))], dots, queries, far
    )
    coded = lax.all_to_all(coded, PIPE, 0, 0)
    parts = call(coded_grad_kernel, shape((OWN, EXT), jnp.int16), coded, index, near, far)

    def finish(parts):
        parts = lax.all_to_all(parts.reshape(16, 2, EXT), "z", 0, 0).reshape(OWN, EXT)
        sums, grad = call(
            inner_kernel, [shape((8, 8, 128)), shape((2, PART))], parts, query, tokens, gain
        )
        sums = lax.all_to_all(sums, PIPE, 0, 0)
        return call(
            output_kernel, [shape((TOKENS, PART)), shape((1,), jnp.int32)],
            sums, grad, query, stat, tokens, gain, far_outs=(0, 1),
            scratch=[
                pltpu.VMEM((TOKENS, PART), f32), pltpu.SMEM((1,), jnp.int32), pltpu.SemaphoreType.DMA((5,))
            ],
        )

    def repeat(state):
        dots = jnp.sum(lax.all_to_all(jnp.broadcast_to(state[2], (8, BANK, 128)), PIPE, 0, 0), axis=0)
        parts = call(exact_grad_kernel, shape((OWN, EXT), jnp.int16), dots, index, near, far)
        return (*finish(parts), dots)

    out = lax.while_loop(lambda state: state[1][0] > 0, repeat, (*finish(parts), exact))[0]
    return out.reshape(2, SEQ, PART)


def solution(mesh):
    fine = Mesh(mesh.devices.reshape(2, 16, 2, 4, 2), ("xh", "z", "c", "y", "xl"))
    dp = ("xh", "z", "c")
    placed = (P(dp, None, PIPE), P(PIPE), P(dp, PIPE), P(dp, PIPE), P(), P(), P())
    return jax.shard_map(
        shards, mesh=fine, in_specs=placed, out_specs=P(dp, None, PIPE), check_vma=False
    )
```
